32 devices in a mesh: box: 2 (over y), gy: 4 (over z), gz: 4 (over x, core).
Axes of the slice: x: 2, y: 2, z: 4, core: 2. Of those that a mesh axis runs over, the one named last changes fastest.
Arguments:
- velocity: float32 [2, 3, 32, 64, 512], P('box', None, 'gz', 'gy'), may hold values from -6 to 6
- turbine_cells: int32 [4, 4, 512], P('gz', 'gy'), may hold values from 0 to 65535, as said below
- turbine_count: int32 [4, 4], P('gz', 'gy'), may hold values from 0 to 512, as said below
- fringe_start: int32 [1], replicated, may hold values from 0 to 384
Outputs:
- advanced: float32 [2, 3, 32, 64, 512], P('box', None, 'gz', 'gy')
The draws below stay inside these ranges and needn't reach their ends.
Inputs may be any that keep to these rules, and one draw needn't show every extreme that they name: `turbine_cells`: flat indices into one device's block of 8 x 16 x 512 cells; cells may repeat. `turbine_count`: some device block has all 512 slots live; others have any number.
All inputs are finite; a program needn't handle non-finite values.
Results may differ from the reference program's by a relative error of at most 0.0003.
Values sent between devices are 32-bit elements; how exact they have to be, the bound alone decides.
No kernel may reach another device: no remote copies, remote signals or barrier semaphores. Data moves between devices by JAX's collectives and lax.ppermute only.
A program may use at most 64 MiB of HBM per device.

```python
import jax
import jax.numpy as jnp
from jax import lax

CZ = 8
CY = 16
NX = 512
FW = 128
TURB = 512
NZ = 32
NY = 64


def draw_turbine_cells(key, part):
    return jax.random.randint(key, (NZ // CZ, NY // CY, TURB), 0, CZ * CY * NX).astype(jnp.int32)


def draw_turbine_count(key, part):
    grid_z = NZ // CZ
    grid_y = NY // CY
    counts = jax.random.randint(jax.random.fold_in(key, 3), (grid_z * grid_y,), 0, TURB + 1)
    chosen = jax.random.randint(jax.random.fold_in(key, 7), (), 0, grid_z * grid_y)
    counts = counts.at[chosen].set(TURB)
    return counts.reshape(grid_z, grid_y).astype(jnp.int32)


def block_levels(stream_key, extent, split, least, top_value):
    def one(dim, shards_of):
        steps = jax.random.uniform(jax.random.fold_in(jax.random.fold_in(stream_key, 6), dim), (shards_of,), jnp.float32, least / len(split), top_value / len(split))
        return jnp.repeat(jnp.exp(steps), extent[dim] // shards_of).reshape((-1,) + (1,) * (len(extent) - dim - 1))

    gain = one(*split[0])
    for cut in split[1:]:
        gain = gain * one(*cut)
    return gain


def noise(key, extent, deviation, most, split=(), held_as=jnp.bfloat16):
    gain = block_levels(key, extent, split, -0.22, 0.18) if split else 1.0
    drawn = jax.random.normal(key, extent, jnp.float32) * deviation * gain
    return jnp.minimum(jnp.maximum(drawn, -most), most).astype(held_as)


def setup_inputs(seed: int = 0) -> dict:
    splits = jax.random.split(jax.random.key(seed), 5)
    velocity = noise(splits[0], (2, 3, NZ, NY, NX), 1.0, 6.0, ((0, 2), (2, 4), (3, 4)), jnp.float32)
    turbine_cells = draw_turbine_cells(jax.random.fold_in(splits[4], 71), 0)
    turbine_count = draw_turbine_count(jax.random.fold_in(splits[4], 71), 0)
    fringe_start = jax.random.randint(splits[3], (1,), 0, NX - FW + 1).astype(jnp.int32)
    return {"velocity": velocity, "turbine_cells": turbine_cells, "turbine_count": turbine_count, "fringe_start": fringe_start}


smag_coef = 0.1024
drag_coef = 0.665
time_step = 0.2
tau_table = ((0, 3, 4), (3, 1, 5), (4, 5, 2))
pair_table = ((0, 0), (1, 1), (2, 2), (0, 1), (0, 2), (1, 2))

def xdiff(field):
    return (jnp.roll(field, -1, -1) - jnp.roll(field, 1, -1)) * 0.5

def sdiff(field, axis):
    count = field.shape[axis]
    return (lax.slice_in_dim(field, 2, count, axis=axis) - lax.slice_in_dim(field, 0, count - 2, axis=axis)) * 0.5

def stress(grads):
    rates = [0.5 * (grads[j][i] + grads[i][j]) for i, j in pair_table]
    squares = rates[0] * rates[0] + rates[1] * rates[1] + rates[2] * rates[2]
    squares = squares + 2.0 * (rates[3] * rates[3] + rates[4] * rates[4] + rates[5] * rates[5])
    visc = smag_coef * jnp.sqrt(2.0 * squares)
    return jnp.stack([2.0 * visc * rate for rate in rates])

def divergence(tau_x, tau_y, tau_z):
    parts = []
    for i in range(3):
        term = xdiff(tau_x[tau_table[i][0]])
        term = term + sdiff(tau_y[tau_table[i][1]], 1)
        term = term + sdiff(tau_z[tau_table[i][2]], 0)
        parts.append(term)
    return jnp.stack(parts)

def advection(center, grads):
    return center[0] * grads[0] + center[1] * grads[1] + center[2] * grads[2]

def pad_span(field):
    return jnp.concatenate([field[:, :, -1:], field, field[:, :, :1]], axis=2)

def pad_vertical(field):
    return jnp.pad(field, ((0, 0), (1, 1), (0, 0), (0, 0)))

def block_drag(flat, cells, count):
    vals = flat[cells]
    live = jnp.arange(cells.shape[0]) < count
    force = jnp.where(live, -drag_coef * vals * jnp.abs(vals), 0.0)
    return jnp.zeros_like(flat).at[cells].add(force)

def main_drag(ux, turbine_cells, turbine_count):
    grid_z = NZ // CZ
    grid_y = NY // CY
    blocks = ux.reshape(grid_z, CZ, grid_y, CY, NX).transpose(0, 2, 1, 3, 4).reshape(grid_z, grid_y, CZ * CY * NX)
    forces = jax.vmap(jax.vmap(block_drag))(blocks, turbine_cells, turbine_count)
    return forces.reshape(grid_z, grid_y, CZ, CY, NX).transpose(0, 2, 1, 3, 4).reshape(NZ, NY, NX)

def rhs(field, drag_x):
    grads = [xdiff(field), sdiff(pad_span(field), 2), sdiff(pad_vertical(field), 1)]
    tau = stress(grads)
    div = divergence(tau, pad_span(tau), pad_vertical(tau))
    result = div - advection(field, grads)
    return result.at[0].add(drag_x)

def rates_both(vel, turbine_cells, turbine_count):
    prec = rhs(vel[0], jnp.zeros_like(vel[0, 0]))
    main = rhs(vel[1], main_drag(vel[1, 0], turbine_cells, turbine_count))
    return jnp.stack([prec, main])

def blend(vel, start):
    cols = jnp.arange(NX)
    inside = (cols >= start) & (cols < start + FW)
    mixed = jnp.where(inside, 0.5 * (vel[1] + vel[0]), vel[1])
    return jnp.stack([vel[0], mixed])

def reference(velocity, turbine_cells, turbine_count, fringe_start):
    start = fringe_start[0]
    first = blend(velocity + time_step * rates_both(velocity, turbine_cells, turbine_count), start)
    second = blend(0.75 * velocity + 0.25 * (first + time_step * rates_both(first, turbine_cells, turbine_count)), start)
    third = 1.0 / 3.0 * velocity + 2.0 / 3.0 * (second + time_step * rates_both(second, turbine_cells, turbine_count))
    return blend(third, start)
```

```python
import functools

import jax
import jax.numpy as jnp
from jax import lax
from jax.experimental import pallas as pl
from jax.experimental.pallas import tpu as pltpu
from jax.sharding import PartitionSpec as P

FW = 128
LANES = 128
HALO = 6
YOFF = 8
MARGIN = 64

smag_coef = 0.1024
drag_coef = 0.665
time_step = 0.2
VMEM_LIMIT = 60 * 1024 * 1024


def corner_rows():
    offset, table = 0, []
    for distance in range(1, HALO):
        table.append((distance, HALO - distance, offset))
        offset += HALO - distance
    return table, offset


def whole_vmem(count):
    return [pl.BlockSpec(memory_space=pltpu.VMEM)] * count


def call(kernel, outs, ins, smem, scratch=()):
    specs = [
        pl.BlockSpec(memory_space=pltpu.SMEM if i < smem else pltpu.VMEM) for i in range(len(ins))
    ]
    return pl.pallas_call(
        kernel,
        out_shape=[jax.ShapeDtypeStruct(shape, jnp.float32) for shape in outs],
        in_specs=specs,
        out_specs=whole_vmem(len(outs)),
        scratch_shapes=list(scratch),
        compiler_params=pltpu.CompilerParams(vmem_limit_bytes=VMEM_LIMIT),
    )(*ins)


def pack_own(dims, scal, u, fringe, up, down):
    tiles, depth, width = dims
    first = scal[0]
    lane0 = scal[1]
    lane = lax.broadcasted_iota(jnp.int32, (width, LANES), 1)
    picked = [lax.rem(first + k, tiles) for k in range(3)]
    for c in range(3):
        for z in range(depth):
            rows = [u[c, z, :, pl.ds(pl.multiple_of(p * LANES, LANES), LANES)] for p in picked]
            for k in range(2):
                at = ((c * 2 + k) * depth + z) * width
                fringe[pl.ds(at, width), :] = jnp.where(lane >= lane0, rows[k], rows[k + 1])
    for c in range(3):
        for t in range(tiles):
            for z in range(depth):
                at = ((c * tiles + t) * depth + z) * HALO
                cols = pl.ds(t * LANES, LANES)
                up[pl.ds(at, HALO), :] = u[c, z, width - HALO :, cols]
                down[pl.ds(at, HALO), :] = u[c, z, :HALO, cols]


def pack_second(dims, u, fringe, fup, fdown, above, below):
    tiles, depth, width = dims
    for c in range(3):
        for k in range(2):
            for z in range(depth):
                at = ((c * 2 + k) * depth + z) * HALO
                src = ((c * 2 + k) * depth + z) * width
                fup[pl.ds(at, HALO), :] = fringe[pl.ds(src + width - HALO, HALO), :]
                fdown[pl.ds(at, HALO), :] = fringe[pl.ds(src, HALO), :]
        for t in range(tiles + 2):
            for h in range(HALO):
                at = ((c * (tiles + 2) + t) * HALO + h) * width
                for out, z in ((above, depth - HALO + h), (below, h)):
                    if t < tiles:
                        value = u[c, z, :, pl.ds(t * LANES, LANES)]
                    else:
                        value = fringe[pl.ds(((c * 2 + t - tiles) * depth + z) * width, width), :]
                    out[pl.ds(at, width), :] = value


def pack_corners(dims, left, right, fleft, fright, above, below):
    tiles, depth, _ = dims
    table, total = corner_rows()
    for c in range(3):
        for t in range(tiles + 2):
            for side in range(2):
                for distance, rows, offset in table:
                    at = ((c * (tiles + 2) + t) * 2 + side) * total + offset
                    for out, z in ((above, depth - distance), (below, distance - 1)):
                        if t < tiles:
                            src, row = (left, right)[side], ((c * tiles + t) * depth + z) * HALO
                        else:
                            src, row = (fleft, fright)[side], ((c * 2 + t - tiles) * depth + z) * HALO
                        row = row + (HALO - rows if side == 0 else 0)
                        out[pl.ds(at, rows), :] = src[pl.ds(row, rows), :]


def multiplicity(dims, lists, out):
    tiles, depth, width = dims
    slots = lists.shape[1]
    reach = HALO - 2
    rows = width + 2 * reach
    levels = depth + 2 * reach
    columns = tiles * LANES
    row_iota = lax.broadcasted_iota(jnp.int32, (levels * rows, slots), 0)
    col_iota = lax.broadcasted_iota(jnp.int32, (columns, slots), 0)
    total = jnp.zeros((levels * rows, columns), jnp.float32)
    for index in range(9):
        oz, oy = index // 3 - 1, index % 3 - 1
        cell = lists[index : index + 1, :]
        x = cell % columns
        y = cell // columns % width + oy * width + reach
        z = cell // (columns * width) + oz * depth + reach
        fits = (cell >= 0) & (y >= 0) & (y < rows) & (z >= 0) & (z < levels)
        row = jnp.where(fits, z * rows + y, -1)
        one = (row_iota == row).astype(jnp.float32).astype(jnp.bfloat16)
        two = (col_iota == x).astype(jnp.float32).astype(jnp.bfloat16)
        total = total + lax.dot_general(
            one, two, (((1,), (1,)), ((), ())), preferred_element_type=jnp.float32
        )
    for t in range(tiles):
        out[t] = total[:, t * LANES : (t + 1) * LANES].reshape(levels, rows, LANES)


def xdiff(value, first, last, nleft, nright):
    ahead = pltpu.roll(value, LANES - 1, 2)
    behind = pltpu.roll(value, 1, 2)
    parts = []
    for i in range(value.shape[0]):
        right = jnp.where(last, ahead[nright[i]], ahead[i])
        left = jnp.where(first, behind[nleft[i]], behind[i])
        parts.append(right - left)
    return jnp.stack(parts)


def tau_tile(src, tau, part, z, y0, span, seam, inside, keep_part):
    first, last, nleft, nright = seam
    here = pl.ds(y0, 8)
    u = [src[c, span, z, here, :] for c in range(3)]
    gx = [xdiff(v, first, last, nleft, nright) for v in u]
    gy = [
        src[c, span, z, pl.ds(y0 + 1, 8), :] - src[c, span, z, pl.ds(y0 - 1, 8), :]
        for c in range(3)
    ]
    gz = [src[c, span, z + 1, here, :] - src[c, span, z - 1, here, :] for c in range(3)]
    xy = gx[1] + gy[0]
    xz = gx[2] + gz[0]
    yz = gy[2] + gz[1]
    diag = gx[0] * gx[0] + gy[1] * gy[1] + gz[2] * gz[2]
    off = xy * xy + xz * xz + yz * yz
    visc = jnp.sqrt(0.5 * diag + 0.25 * off) * inside
    half = visc * 0.5
    for k, value in enumerate(
        (visc * gx[0], visc * gy[1], visc * gz[2], half * xy, half * xz, half * yz)
    ):
        tau[k, span, z, here, :] = value
    if keep_part:
        scaled = [v * (-0.5 * time_step) for v in u]
        for c in range(3):
            part[c, span, z, here, :] = u[c] + (
                scaled[0] * gx[c] + scaled[1] * gy[c] + scaled[2] * gz[c]
            )


TAU = ((0, 3, 4), (3, 1, 5), (4, 5, 2))


def out_tile(src, base, tau, part, z, y0, span, seam, weights):
    first, last, nleft, nright = seam
    here = pl.ds(y0, 8)
    keep, take = weights
    results = []
    for c in range(3):
        div = xdiff(tau[TAU[c][0], span, z, here, :], first, last, nleft, nright)
        div = div + (
            tau[TAU[c][1], span, z, pl.ds(y0 + 1, 8), :]
            - tau[TAU[c][1], span, z, pl.ds(y0 - 1, 8), :]
        )
        div = div + (tau[TAU[c][2], span, z + 1, here, :] - tau[TAU[c][2], span, z - 1, here, :])
        value = part[c, span, z, here, :] * take + div * (take * time_step * 0.5 * smag_coef)
        if keep:
            value = value + keep * base[c, span, z, here, :]
        results.append(value)
    return results


def step_kernel(
    dims, scal, u, left, right, fringe, fleft, fright, under, over, cunder, cover, count, out,
    u0, u1, u2, tau, part,
):
    tiles, depth, width = dims
    start, lane0, main, bottom, top = (scal[i] for i in (2, 1, 3, 4, 5))
    table, total = corner_rows()
    all_tiles = tiles + 2
    for c in range(3):
        for t in range(tiles):
            cols = pl.ds(t * LANES, LANES)
            for z in range(depth):
                at = ((c * tiles + t) * depth + z) * HALO
                u0[c, t, z + HALO, pl.ds(YOFF, width), :] = u[c, z, :, cols]
                u0[c, t, z + HALO, pl.ds(YOFF - HALO, HALO), :] = left[pl.ds(at, HALO), :]
                u0[c, t, z + HALO, pl.ds(YOFF + width, HALO), :] = right[pl.ds(at, HALO), :]
        for k in range(2):
            for z in range(depth):
                at = (c * 2 + k) * depth + z
                rows = pl.ds(at * HALO, HALO)
                u0[c, tiles + k, z + HALO, pl.ds(YOFF, width), :] = fringe[pl.ds(at * width, width), :]
                u0[c, tiles + k, z + HALO, pl.ds(YOFF - HALO, HALO), :] = fleft[rows, :]
                u0[c, tiles + k, z + HALO, pl.ds(YOFF + width, HALO), :] = fright[rows, :]
        for t in range(all_tiles):
            for h in range(HALO):
                rows = pl.ds(((c * all_tiles + t) * HALO + h) * width, width)
                u0[c, t, h, pl.ds(YOFF, width), :] = under[rows, :]
                u0[c, t, HALO + depth + h, pl.ds(YOFF, width), :] = over[rows, :]
            for side in range(2):
                for distance, rows, offset in table:
                    at = ((c * all_tiles + t) * 2 + side) * total + offset
                    y = YOFF - rows if side == 0 else YOFF + width
                    u0[c, t, HALO - distance, pl.ds(y, rows), :] = cunder[pl.ds(at, rows), :]
                    u0[c, t, HALO + depth + distance - 1, pl.ds(y, rows), :] = cover[pl.ds(at, rows), :]

    def clear(z):
        for c in range(3):
            u0[c, :, z] = jnp.zeros(u0.shape[1:2] + u0.shape[3:], jnp.float32)

    @pl.when(bottom == 1)
    def _():
        lax.fori_loop(0, HALO, lambda i, _: clear(i), None)

    @pl.when(top == 1)
    def _():
        lax.fori_loop(0, HALO, lambda i, _: clear(HALO + depth + i), None)

    lane = lax.broadcasted_iota(jnp.int32, (8, LANES), 1)
    order = list(range(tiles))
    main_seam = (lane == 0, lane == LANES - 1, order[-1:] + order[:-1], order[1:] + order[:1])
    window_seam = (lane == lane0, lane == lax.rem(lane0 + LANES - 1, LANES), [1, 0], [1, 0])
    main_span, window_span = slice(0, tiles), slice(tiles, tiles + 2)

    def inside_of(z):
        below = (z < HALO) & (bottom == 1)
        above = (z >= HALO + depth) & (top == 1)
        return jnp.where(below | above, 0.0, 1.0)

    def loop(low, high, body):
        def step(z, _):
            body(z)

        lax.fori_loop(low, high, step, None)

    def tau_stage(src, margin, span, seam):
        rows = list(range(YOFF - margin, YOFF + width + margin - 8, 8)) + [YOFF + width + margin - 8]
        fewer = list(range(YOFF - margin + 1, YOFF + width + margin - 9, 8)) + [YOFF + width + margin - 9]

        def body(starts, z):
            for y0 in starts:
                tau_tile(src, tau, part, z, y0, span, seam, inside_of(z), True)

        loop(HALO, HALO + depth, functools.partial(body, rows))
        loop(HALO - margin, HALO, functools.partial(body, fewer))
        loop(HALO + depth, HALO + depth + margin, functools.partial(body, fewer))

    def out_stage(src, dst, margin, weights, span, seam, blended):
        rows = list(range(YOFF - margin, YOFF + width + margin - 8, 8)) + [YOFF + width + margin - 8]
        reach = HALO - 2

        def body(z):
            inside = inside_of(z)
            for y0 in rows:
                here = pl.ds(y0, 8)
                values = out_tile(src, u0, tau, part, z, y0, span, seam, weights)
                if blended:
                    ux = src[0, span, z, here, :]
                    times = count[:, z - HALO + reach, pl.ds(y0 - YOFF + reach, 8), :]
                    factor = jnp.where(main == 1, -drag_coef * time_step * weights[1], 0.0)
                    values[0] = values[0] + (times * factor) * (ux * jnp.abs(ux))
                for c in range(3):
                    value = values[c]
                    if blended:
                        near = dst[c, tiles, z, here, :]
                        far = dst[c, tiles + 1, z, here, :]
                        parts = []
                        for t in range(tiles):
                            col = lane + t * LANES
                            mask = (col >= start) & (col < start + FW) & (main == 1)
                            other = jnp.where(col < start + MARGIN, near, far)
                            parts.append(jnp.where(mask, 0.5 * (value[t] + other), value[t]))
                        value = jnp.stack(parts)
                    dst[c, span, z, here, :] = value * inside

        loop(HALO - margin, HALO + depth + margin, body)

    stages = (
        (u0, u1, HALO - 1, (0.0, 1.0)),
        (u1, u2, HALO - 3, (0.75, 0.25)),
        (u2, u1, HALO - 5, (1.0 / 3.0, 2.0 / 3.0)),
    )
    for src, dst, margin, weights in stages:

        @pl.when(main == 1)
        def _():
            tau_stage(src, margin, window_span, window_seam)
            out_stage(src, dst, margin - 1, weights, window_span, window_seam, False)

        tau_stage(src, margin, main_span, main_seam)
        out_stage(src, dst, margin - 1, weights, main_span, main_seam, True)
    for c in range(3):
        for t in range(tiles):
            for z in range(depth):
                out[c, z, :, pl.ds(t * LANES, LANES)] = u1[c, t, z + HALO, pl.ds(YOFF, width), :]


def around(axis, by):
    count = lax.axis_size(axis)
    return [(i, (i + by) % count) for i in range(count)]


def per_device(velocity, turbine_cells, turbine_count, fringe_start):
    u = velocity[0]
    _, depth, width, columns = u.shape
    tiles = columns // LANES
    dims = (tiles, depth, width)
    start = fringe_start[0]
    origin = (start + columns - MARGIN) % columns
    gz, gy = lax.axis_index("gz"), lax.axis_index("gy")
    nz, ny = lax.axis_size("gz"), lax.axis_size("gy")
    scal = jnp.stack(
        [
            origin // LANES,
            origin % LANES,
            start,
            (lax.axis_index("box") == 1).astype(jnp.int32),
            (gz == 0).astype(jnp.int32),
            (gz == nz - 1).astype(jnp.int32),
        ]
    ).astype(jnp.int32)

    slots = turbine_cells.shape[-1]
    cells = turbine_cells.reshape(slots)
    cells = jnp.where(jnp.arange(slots) < turbine_count.reshape(()), cells, -1)
    every = lax.all_gather(cells, ("gy", "gz"))
    lists = []
    for oz in (-1, 0, 1):
        for oy in (-1, 0, 1):
            z = gz + oz
            row = lax.dynamic_index_in_dim(
                every, (gy + oy) % ny * nz + jnp.clip(z, 0, nz - 1), keepdims=False
            )
            lists.append(jnp.where((z >= 0) & (z < nz), row, -1))
    lists = jnp.stack(lists)

    halo_rows = 3 * tiles * depth * HALO
    window_rows = 3 * 2 * depth * HALO
    level_rows = 3 * (tiles + 2) * HALO * width
    corner = 3 * (tiles + 2) * 2 * corner_rows()[1]
    corner = (corner + 7) // 8 * 8

    fringe, up, down = call(
        functools.partial(pack_own, dims),
        [(3 * 2 * depth * width, LANES), (halo_rows, LANES), (halo_rows, LANES)],
        (scal, u),
        1,
    )
    fringe = lax.ppermute(fringe, "box", [(0, 1), (1, 0)])
    left = lax.ppermute(up, "gy", around("gy", 1))
    right = lax.ppermute(down, "gy", around("gy", -1))
    fup, fdown, above, below = call(
        functools.partial(pack_second, dims),
        [(window_rows, LANES), (window_rows, LANES), (level_rows, LANES), (level_rows, LANES)],
        (u, fringe),
        0,
    )
    fleft = lax.ppermute(fup, "gy", around("gy", 1))
    fright = lax.ppermute(fdown, "gy", around("gy", -1))
    under = lax.ppermute(above, "gz", around("gz", 1))
    over = lax.ppermute(below, "gz", around("gz", -1))
    cabove, cbelow = call(
        functools.partial(pack_corners, dims),
        [(corner, LANES), (corner, LANES)],
        (left, right, fleft, fright),
        0,
    )
    cunder = lax.ppermute(cabove, "gz", around("gz", 1))
    cover = lax.ppermute(cbelow, "gz", around("gz", -1))

    reach = HALO - 2
    (count,) = call(
        functools.partial(multiplicity, dims),
        [(tiles, depth + 2 * reach, width + 2 * reach, LANES)],
        (lists,),
        0,
    )
    ext = (tiles + 2, depth + 2 * HALO, width + 2 * YOFF, LANES)
    (out,) = call(
        functools.partial(step_kernel, dims),
        [u.shape],
        (scal, u, left, right, fringe, fleft, fright, under, over, cunder, cover, count),
        1,
        [pltpu.VMEM((n,) + ext, jnp.float32) for n in (3, 3, 3, 6, 3)],
    )
    return out[None]


def solution(mesh):
    placed = (P("box", None, "gz", "gy", None), P("gz", "gy", None), P("gz", "gy"), P())
    return jax.shard_map(
        per_device,
        mesh=mesh,
        in_specs=placed,
        out_specs=P("box", None, "gz", "gy", None),
        check_vma=False,
    )
```

```python
import functools

import jax
import jax.numpy as jnp
from jax import lax
from jax.experimental import pallas as pl
from jax.experimental.pallas import tpu as pltpu
from jax.sharding import PartitionSpec as P

FW = 128
LANES = 128
HALO = 6
YOFF = 8
MARGIN = 64

smag_coef = 0.1024
drag_coef = 0.665
time_step = 0.2
LISTED = 4


def corner_rows():
    offset, table = 0, []
    for distance in range(1, HALO):
        table.append((distance, HALO - distance, offset))
        offset += HALO - distance
    return table, offset


def whole_vmem(count):
    return [pl.BlockSpec(memory_space=pltpu.VMEM)] * count


def call(kernel, outs, ins, smem, limit, cost, scratch=()):
    specs = [
        pl.BlockSpec(memory_space=pltpu.SMEM if i < smem else pltpu.VMEM) for i in range(len(ins))
    ]
    return pl.pallas_call(
        kernel,
        out_shape=[jax.ShapeDtypeStruct(shape, jnp.float32) for shape in outs],
        in_specs=specs,
        out_specs=whole_vmem(len(outs)),
        scratch_shapes=list(scratch),
        compiler_params=pltpu.CompilerParams(vmem_limit_bytes=limit * 1024 * 1024),
        cost_estimate=pl.CostEstimate(flops=cost, bytes_accessed=cost, transcendentals=0),
    )(*ins)


def place(start, columns):
    origin = lax.rem(start + columns - MARGIN, columns)
    return origin // LANES, lax.rem(origin, LANES)


def pack_own(dims, start, live, cells, u, fringe, up, down, above, below):
    tiles, depth, width = dims
    first, lane0 = place(start[0], tiles * LANES)
    lane = lax.broadcasted_iota(jnp.int32, (width, LANES), 1)
    picked = [lax.rem(first + k, tiles) for k in range(3)]
    slot = lax.broadcasted_iota(jnp.int32, (1, LANES), 1)
    for k in range(LISTED):
        row = cells[0, :, pl.ds(k * LANES, LANES)]
        row = jnp.where(slot + k * LANES < live[0, 0], row, -1).astype(jnp.float32)
        for out in (above, below):
            out[pl.ds(3 * tiles * HALO * width + k, 1), :] = row
    for c in range(3):
        for t in range(tiles):
            cols = pl.ds(t * LANES, LANES)
            for z in range(depth):
                at = ((c * tiles + t) * depth + z) * HALO
                up[pl.ds(at, HALO), :] = u[c, z, width - HALO :, cols]
                down[pl.ds(at, HALO), :] = u[c, z, :HALO, cols]
            for h in range(HALO):
                at = ((c * tiles + t) * HALO + h) * width
                above[pl.ds(at, width), :] = u[c, depth - HALO + h, :, cols]
                below[pl.ds(at, width), :] = u[c, h, :, cols]
    for c in range(3):
        for z in range(depth):
            rows = [u[c, z, :, pl.ds(pl.multiple_of(p * LANES, LANES), LANES)] for p in picked]
            for k in range(2):
                at = ((c * 2 + k) * depth + z) * width
                fringe[pl.ds(at, width), :] = jnp.where(lane >= lane0, rows[k], rows[k + 1])


def pack_window(dims, own, under, over, fringe, fup, fdown, above, below):
    tiles, depth, width = dims
    listed = 3 * tiles * HALO * width
    for k, source in enumerate((under, own, over)):
        for out in (fup, fdown):
            out[pl.ds(3 * 2 * depth * HALO + k * LISTED, LISTED), :] = source[pl.ds(listed, LISTED), :]
    for c in range(3):
        for k in range(2):
            for z in range(depth):
                at = ((c * 2 + k) * depth + z) * HALO
                src = ((c * 2 + k) * depth + z) * width
                fup[pl.ds(at, HALO), :] = fringe[pl.ds(src + width - HALO, HALO), :]
                fdown[pl.ds(at, HALO), :] = fringe[pl.ds(src, HALO), :]
            for h in range(HALO):
                at = ((c * 2 + k) * HALO + h) * width
                for out, z in ((above, depth - HALO + h), (below, h)):
                    src = ((c * 2 + k) * depth + z) * width
                    out[pl.ds(at, width), :] = fringe[pl.ds(src, width), :]


def pack_corners(dims, left, right, fleft, fright, above, below):
    tiles, depth, _ = dims
    table, total = corner_rows()
    for c in range(3):
        for t in range(tiles + 2):
            for side in range(2):
                for distance, rows, offset in table:
                    at = ((c * (tiles + 2) + t) * 2 + side) * total + offset
                    for out, z in ((above, depth - distance), (below, distance - 1)):
                        if t < tiles:
                            src, row = (left, right)[side], ((c * tiles + t) * depth + z) * HALO
                        else:
                            src, row = (fleft, fright)[side], ((c * 2 + t - tiles) * depth + z) * HALO
                        row = row + (HALO - rows if side == 0 else 0)
                        out[pl.ds(at, rows), :] = src[pl.ds(row, rows), :]


def multiplicity(dims, own, under, over, fleft, fright, out):
    tiles, depth, width = dims
    reach = HALO - 2
    rows = width + 2 * reach
    levels = depth + 2 * reach
    columns = tiles * LANES
    bottom = lax.axis_index("gz") == 0
    top = lax.axis_index("gz") == lax.axis_size("gz") - 1
    row_iota = lax.broadcasted_iota(jnp.int32, (levels * rows, LANES), 0)
    col_iota = lax.broadcasted_iota(jnp.int32, (columns, LANES), 0)
    level_at, window_at = 3 * tiles * HALO * width, 3 * 2 * depth * HALO
    total = jnp.zeros((levels * rows, columns), jnp.float32)
    for index in range(9):
        oz, oy = index // 3 - 1, index % 3 - 1
        if oy == 0:
            source, at = (under, own, over)[oz + 1], level_at
        else:
            source, at = (fleft, None, fright)[oy + 1], window_at + (oz + 1) * LISTED
        for k in range(LISTED):
            cell = source[pl.ds(at + k, 1), :].astype(jnp.int32)
            x = cell % columns
            y = cell // columns % width + oy * width + reach
            z = cell // (columns * width) + oz * depth + reach
            fits = (cell >= 0) & (y >= 0) & (y < rows) & (z >= 0) & (z < levels)
            if oz < 0:
                fits = fits & jnp.logical_not(bottom)
            if oz > 0:
                fits = fits & jnp.logical_not(top)
            row = jnp.where(fits, z * rows + y, -1)
            one = (row_iota == row).astype(jnp.float32).astype(jnp.bfloat16)
            two = (col_iota == x).astype(jnp.float32).astype(jnp.bfloat16)
            total = total + lax.dot_general(
                one, two, (((1,), (1,)), ((), ())), preferred_element_type=jnp.float32
            )
    for t in range(tiles):
        out[t] = total[:, t * LANES : (t + 1) * LANES].reshape(levels, rows, LANES)


def xdiff(value, first, last, nleft, nright):
    ahead = pltpu.roll(value, LANES - 1, 2)
    behind = pltpu.roll(value, 1, 2)
    parts = []
    for i in range(value.shape[0]):
        right = jnp.where(last, ahead[nright[i]], ahead[i])
        left = jnp.where(first, behind[nleft[i]], behind[i])
        parts.append(right - left)
    return jnp.stack(parts)


def tau_tile(src, tau, part, z, y0, span, seam, inside, keep_part):
    first, last, nleft, nright = seam
    here = pl.ds(y0, 8)
    u = [src[c, span, z, here, :] for c in range(3)]
    gx = [xdiff(v, first, last, nleft, nright) for v in u]
    gy = [
        src[c, span, z, pl.ds(y0 + 1, 8), :] - src[c, span, z, pl.ds(y0 - 1, 8), :]
        for c in range(3)
    ]
    gz = [src[c, span, z + 1, here, :] - src[c, span, z - 1, here, :] for c in range(3)]
    xy = gx[1] + gy[0]
    xz = gx[2] + gz[0]
    yz = gy[2] + gz[1]
    diag = gx[0] * gx[0] + gy[1] * gy[1] + gz[2] * gz[2]
    off = xy * xy + xz * xz + yz * yz
    visc = jnp.sqrt(0.5 * diag + 0.25 * off)
    if inside is not None:
        visc = visc * inside
    half = visc * 0.5
    for k, value in enumerate(
        (visc * gx[0], visc * gy[1], visc * gz[2], half * xy, half * xz, half * yz)
    ):
        tau[k, span, z, here, :] = value
    if keep_part:
        scaled = [v * (-0.5 * time_step) for v in u]
        for c in range(3):
            part[c, span, z, here, :] = u[c] + (
                scaled[0] * gx[c] + scaled[1] * gy[c] + scaled[2] * gz[c]
            )


TAU = ((0, 3, 4), (3, 1, 5), (4, 5, 2))


def out_tile(src, base, tau, part, z, y0, span, seam, weights):
    first, last, nleft, nright = seam
    here = pl.ds(y0, 8)
    keep, take = weights
    results = []
    for c in range(3):
        div = xdiff(tau[TAU[c][0], span, z, here, :], first, last, nleft, nright)
        div = div + (
            tau[TAU[c][1], span, z, pl.ds(y0 + 1, 8), :]
            - tau[TAU[c][1], span, z, pl.ds(y0 - 1, 8), :]
        )
        div = div + (tau[TAU[c][2], span, z + 1, here, :] - tau[TAU[c][2], span, z - 1, here, :])
        value = part[c, span, z, here, :] * take + div * (take * time_step * 0.5 * smag_coef)
        if keep:
            value = value + keep * base[c, span, z, here, :]
        results.append(value)
    return results


def step_kernel(
    dims, first_column, u, left, right, fringe, fleft, fright, under, over, funder, fover,
    cunder, cover, count, out, u0, u1, u2, tau, part,
):
    tiles, depth, width = dims
    start = first_column[0]
    _, lane0 = place(start, tiles * LANES)
    main = lax.axis_index("box")
    bottom = (lax.axis_index("gz") == 0).astype(jnp.int32)
    top = (lax.axis_index("gz") == lax.axis_size("gz") - 1).astype(jnp.int32)
    table, total = corner_rows()
    all_tiles = tiles + 2
    for c in range(3):
        for t in range(tiles):
            cols = pl.ds(t * LANES, LANES)
            for z in range(depth):
                at = ((c * tiles + t) * depth + z) * HALO
                u0[c, t, z + HALO, pl.ds(YOFF, width), :] = u[c, z, :, cols]
                u0[c, t, z + HALO, pl.ds(YOFF - HALO, HALO), :] = left[pl.ds(at, HALO), :]
                u0[c, t, z + HALO, pl.ds(YOFF + width, HALO), :] = right[pl.ds(at, HALO), :]
        for k in range(2):
            for z in range(depth):
                at = (c * 2 + k) * depth + z
                rows = pl.ds(at * HALO, HALO)
                u0[c, tiles + k, z + HALO, pl.ds(YOFF, width), :] = fringe[pl.ds(at * width, width), :]
                u0[c, tiles + k, z + HALO, pl.ds(YOFF - HALO, HALO), :] = fleft[rows, :]
                u0[c, tiles + k, z + HALO, pl.ds(YOFF + width, HALO), :] = fright[rows, :]
        for t in range(all_tiles):
            for h in range(HALO):
                lower, upper, at = under, over, (c * tiles + t) * HALO + h
                if t >= tiles:
                    lower, upper, at = funder, fover, (c * 2 + t - tiles) * HALO + h
                rows = pl.ds(at * width, width)
                u0[c, t, h, pl.ds(YOFF, width), :] = lower[rows, :]
                u0[c, t, HALO + depth + h, pl.ds(YOFF, width), :] = upper[rows, :]
            for side in range(2):
                for distance, rows, offset in table:
                    at = ((c * all_tiles + t) * 2 + side) * total + offset
                    y = YOFF - rows if side == 0 else YOFF + width
                    u0[c, t, HALO - distance, pl.ds(y, rows), :] = cunder[pl.ds(at, rows), :]
                    u0[c, t, HALO + depth + distance - 1, pl.ds(y, rows), :] = cover[pl.ds(at, rows), :]

    def clear(z):
        for c in range(3):
            u0[c, :, z] = jnp.zeros(u0.shape[1:2] + u0.shape[3:], jnp.float32)

    @pl.when(bottom == 1)
    def _():
        lax.fori_loop(0, HALO, lambda i, _: clear(i), None)

    @pl.when(top == 1)
    def _():
        lax.fori_loop(0, HALO, lambda i, _: clear(HALO + depth + i), None)

    lane = lax.broadcasted_iota(jnp.int32, (8, LANES), 1)
    order = list(range(tiles))
    main_seam = (lane == 0, lane == LANES - 1, order[-1:] + order[:-1], order[1:] + order[:1])
    window_seam = (lane == lane0, lane == lax.rem(lane0 + LANES - 1, LANES), [1, 0], [1, 0])
    main_span, window_span = slice(0, tiles), slice(tiles, tiles + 2)

    def inside_of(z):
        if HALO <= z < HALO + depth:
            return None
        return 1.0 - (bottom if z < HALO else top).astype(jnp.float32)

    def sweep(margin, body):
        for z in range(HALO - margin, HALO + depth + margin):
            reach = margin - max(HALO - z, z - (HALO + depth - 1), 0)
            stop = YOFF + width + reach - 8
            for y0 in list(range(YOFF - reach, stop, 8)) + [stop]:
                body(z, y0)

    def tau_stage(src, margin, span, seam):
        def body(z, y0):
            tau_tile(src, tau, part, z, y0, span, seam, inside_of(z), True)

        sweep(margin, body)

    def out_stage(src, dst, margin, weights, span, seam, blended):
        reach = HALO - 2

        def body(z, y0):
            here = pl.ds(y0, 8)
            values = out_tile(src, u0, tau, part, z, y0, span, seam, weights)
            if blended:
                ux = src[0, span, z, here, :]
                times = count[:, z - HALO + reach, pl.ds(y0 - YOFF + reach, 8), :]
                factor = jnp.where(main == 1, -drag_coef * time_step * weights[1], 0.0)
                values[0] = values[0] + (times * factor) * (ux * jnp.abs(ux))
            for c in range(3):
                value = values[c]
                if blended:
                    near = dst[c, tiles, z, here, :]
                    far = dst[c, tiles + 1, z, here, :]
                    parts = []
                    for t in range(tiles):
                        col = lane + t * LANES
                        mask = (col >= start) & (col < start + FW) & (main == 1)
                        other = jnp.where(col < start + MARGIN, near, far)
                        parts.append(jnp.where(mask, 0.5 * (value[t] + other), value[t]))
                    value = jnp.stack(parts)
                if inside_of(z) is not None:
                    value = value * inside_of(z)
                dst[c, span, z, here, :] = value

        sweep(margin, body)

    stages = (
        (u0, u1, HALO - 1, (0.0, 1.0)),
        (u1, u2, HALO - 3, (0.75, 0.25)),
        (u2, u1, HALO - 5, (1.0 / 3.0, 2.0 / 3.0)),
    )
    for src, dst, margin, weights in stages:

        @pl.when(main == 1)
        def _():
            tau_stage(src, margin, window_span, window_seam)
            out_stage(src, dst, margin - 1, weights, window_span, window_seam, False)

        tau_stage(src, margin, main_span, main_seam)
        out_stage(src, dst, margin - 1, weights, main_span, main_seam, True)
    for c in range(3):
        for t in range(tiles):
            for z in range(depth):
                out[c, z, :, pl.ds(t * LANES, LANES)] = u1[c, t, z + HALO, pl.ds(YOFF, width), :]


def around(axis, by):
    count = lax.axis_size(axis)
    return [(i, (i + by) % count) for i in range(count)]


def per_device(velocity, turbine_cells, turbine_count, fringe_start):
    u = velocity[0]
    _, depth, width, columns = u.shape
    tiles = columns // LANES
    dims = (tiles, depth, width)

    halo_rows = 3 * tiles * depth * HALO
    level_rows = 3 * tiles * HALO * width + 8
    window_halo_rows = 3 * 2 * depth * HALO + 16
    window_level_rows = 3 * 2 * HALO * width
    corner = 3 * (tiles + 2) * 2 * corner_rows()[1]
    corner = (corner + 7) // 8 * 8

    fringe, up, down, above, below = call(
        functools.partial(pack_own, dims),
        [
            (3 * 2 * depth * width, LANES),
            (halo_rows, LANES),
            (halo_rows, LANES),
            (level_rows, LANES),
            (level_rows, LANES),
        ],
        (fringe_start, turbine_count, turbine_cells, u),
        2,
        12,
        1,
    )
    left = lax.ppermute(up, "gy", around("gy", 1))
    right = lax.ppermute(down, "gy", around("gy", -1))
    under = lax.ppermute(above, "gz", around("gz", 1))
    over = lax.ppermute(below, "gz", around("gz", -1))
    fringe = lax.ppermute(fringe, "box", [(0, 1), (1, 0)])
    fup, fdown, fabove, fbelow = call(
        functools.partial(pack_window, dims),
        [
            (window_halo_rows, LANES),
            (window_halo_rows, LANES),
            (window_level_rows, LANES),
            (window_level_rows, LANES),
        ],
        (above, under, over, fringe),
        0,
        12,
        1,
    )
    fleft = lax.ppermute(fup, "gy", around("gy", 1))
    fright = lax.ppermute(fdown, "gy", around("gy", -1))
    funder = lax.ppermute(fabove, "gz", around("gz", 1))
    fover = lax.ppermute(fbelow, "gz", around("gz", -1))
    cabove, cbelow = call(
        functools.partial(pack_corners, dims),
        [(corner, LANES), (corner, LANES)],
        (left, right, fleft, fright),
        0,
        8,
        1,
    )
    cunder = lax.ppermute(cabove, "gz", around("gz", 1))
    cover = lax.ppermute(cbelow, "gz", around("gz", -1))

    reach = HALO - 2
    (count,) = call(
        functools.partial(multiplicity, dims),
        [(tiles, depth + 2 * reach, width + 2 * reach, LANES)],
        (above, under, over, fleft, fright),
        0,
        12,
        8_000_000,
    )
    ext = (tiles + 2, depth + 2 * HALO, width + 2 * YOFF, LANES)
    (out,) = call(
        functools.partial(step_kernel, dims),
        [u.shape],
        (fringe_start, u, left, right, fringe, fleft, fright, under, over, funder, fover, cunder, cover, count),
        1,
        48,
        8_000_000,
        [pltpu.VMEM((n,) + ext, jnp.float32) for n in (3, 3, 3, 6, 3)],
    )
    return out[None]


def solution(mesh):
    placed = (P("box", None, "gz", "gy", None), P("gz", "gy", None), P("gz", "gy"), P())
    return jax.shard_map(
        per_device,
        mesh=mesh,
        in_specs=placed,
        out_specs=P("box", None, "gz", "gy", None),
        check_vma=False,
    )
```

```python
import functools

import jax
import jax.numpy as jnp
from jax import lax
from jax.experimental import pallas as pl
from jax.experimental.pallas import tpu as pltpu
from jax.sharding import PartitionSpec as P

FW = 128
LANES = 128
HALO = 6
RING = HALO - 2
GROUP = 16

smag_coef = 0.1024
drag_coef = 0.665
time_step = 0.2
LISTED = 4


def corner_rows():
    offset, table = 0, []
    for distance in range(1, HALO):
        table.append((distance, HALO - distance, offset))
        offset += HALO - distance
    return table, offset


def whole_vmem(count):
    return [pl.BlockSpec(memory_space=pltpu.VMEM)] * count


def call(kernel, outs, ins, smem, limit, cost, scratch=()):
    specs = [
        pl.BlockSpec(memory_space=pltpu.SMEM if i < smem else pltpu.VMEM) for i in range(len(ins))
    ]
    return pl.pallas_call(
        kernel,
        out_shape=[jax.ShapeDtypeStruct(shape, jnp.float32) for shape in outs],
        in_specs=specs,
        out_specs=whole_vmem(len(outs)),
        scratch_shapes=list(scratch),
        compiler_params=pltpu.CompilerParams(vmem_limit_bytes=limit * 1024 * 1024),
        cost_estimate=pl.CostEstimate(flops=cost, bytes_accessed=cost, transcendentals=0),
    )(*ins)


def place(start, columns):
    origin = lax.rem(start + columns - HALO, columns)
    return origin // LANES, lax.rem(origin, LANES)


def parity(body):
    even = lax.rem(lax.axis_index("gz"), 2) == 0
    pl.when(even)(functools.partial(body, True))
    pl.when(jnp.logical_not(even))(functools.partial(body, False))


def pack_own(dims, start, live, cells, u, fringe, up, down, first, second):
    tiles, depth, width = dims
    tile0, lane0 = place(start[0], tiles * LANES)
    lane = lax.broadcasted_iota(jnp.int32, (width, LANES), 1)
    offset = lax.rem(lane - lane0 + LANES, LANES)
    picked = [
        pl.ds(pl.multiple_of(lax.rem(tile0 + k, tiles) * LANES, LANES), LANES) for k in range(3)
    ]
    slot = lax.broadcasted_iota(jnp.int32, (1, LANES), 1)
    half = depth // 2
    for zz in range(half):
        packed = None
        for c in range(3):
            for part in range(2):
                z = zz + part * half
                rows = [u[c, z, :, p] for p in picked]
                at = (c * depth + z) * width
                fringe[pl.ds(at, width), :] = jnp.where(lane >= lane0, rows[0], rows[1])
                last = jnp.where(lane >= lane0, rows[1], rows[2])
                group = GROUP * (c * 2 + part)
                if packed is None:
                    packed = last
                else:
                    packed = jnp.where(offset >= group, pltpu.roll(last, group, 1), packed)
        fringe[pl.ds((3 * depth + zz) * width, width), :] = packed
    for c in range(3):
        for t in range(tiles):
            cols = pl.ds(t * LANES, LANES)
            for z in range(depth):
                at = ((c * tiles + t) * depth + z) * HALO
                up[pl.ds(at, HALO), :] = u[c, z, width - HALO :, cols]
                down[pl.ds(at, HALO), :] = u[c, z, :HALO, cols]
    for k in range(LISTED):
        row = cells[0, :, pl.ds(k * LANES, LANES)]
        row = jnp.where(slot + k * LANES < live[0, 0], row, -1).astype(jnp.float32)
        for out in (first, second):
            out[pl.ds(3 * tiles * HALO * width + k, 1), :] = row

    def levels(even):
        above, below = (first, second) if even else (second, first)
        for c in range(3):
            for t in range(tiles):
                cols = pl.ds(t * LANES, LANES)
                for h in range(HALO):
                    at = ((c * tiles + t) * HALO + h) * width
                    above[pl.ds(at, width), :] = u[c, depth - HALO + h, :, cols]
                    below[pl.ds(at, width), :] = u[c, h, :, cols]

    parity(levels)


def pack_window(dims, own, near, far, fringe, fup, fdown, first, second):
    tiles, depth, width = dims
    half = depth // 2
    listed, list_at = 3 * tiles * HALO * width, (3 * depth + half) * HALO
    for k, source in enumerate((near, own, far)):
        for out in (fup, fdown):
            out[pl.ds(list_at + k * LISTED, LISTED), :] = source[pl.ds(listed, LISTED), :]
    for at in range(3 * depth + half):
        fup[pl.ds(at * HALO, HALO), :] = fringe[pl.ds(at * width + width - HALO, HALO), :]
        fdown[pl.ds(at * HALO, HALO), :] = fringe[pl.ds(at * width, HALO), :]
    for out in (first, second):
        for zz in range(half):
            out[pl.ds((3 * HALO + zz) * width, width), :] = fringe[
                pl.ds((3 * depth + zz) * width, width), :
            ]

    def levels(even):
        above, below = (first, second) if even else (second, first)
        for c in range(3):
            for h in range(HALO):
                at = pl.ds((c * HALO + h) * width, width)
                above[at, :] = fringe[pl.ds((c * depth + depth - HALO + h) * width, width), :]
                below[at, :] = fringe[pl.ds((c * depth + h) * width, width), :]

    parity(levels)


def pack_corners(dims, left, right, fleft, fright, fnear, ffar, first, second):
    tiles, depth, _ = dims
    table, total = corner_rows()
    half = depth // 2
    tail = 3 * (tiles + 1) * 2 * total
    for out in (first, second):
        for side, source in enumerate((fleft, fright)):
            out[pl.ds(tail + side * half * HALO, half * HALO), :] = source[
                pl.ds(3 * depth * HALO, half * HALO), :
            ]

    def corners(even):
        above, below = (first, second) if even else (second, first)
        for c in range(3):
            for t in range(tiles + 1):
                for side in range(2):
                    for distance, rows, offset in table:
                        if t < tiles:
                            at = (c * tiles + t) * 2 + side
                            source, row = (left, right)[side], (c * tiles + t) * depth
                        else:
                            at = (3 * tiles + c) * 2 + side
                            source, row = (fleft, fright)[side], c * depth
                        skip = HALO - rows if side == 0 else 0
                        for out, z in ((above, depth - distance), (below, distance - 1)):
                            out[pl.ds(at * total + offset, rows), :] = source[
                                pl.ds((row + z) * HALO + skip, rows), :
                            ]

    parity(corners)


def multiplicity(dims, own, near, far, fleft, fright, out):
    tiles, depth, width = dims
    rows, levels, columns = width + 2 * RING, depth + 2 * RING, tiles * LANES
    place_z, count_z = lax.axis_index("gz"), lax.axis_size("gz")
    step = 1 - 2 * lax.rem(place_z, 2)
    row_iota = lax.broadcasted_iota(jnp.int32, (levels * rows, LANES), 0)
    col_iota = lax.broadcasted_iota(jnp.int32, (columns, LANES), 0)
    level_at, window_at = 3 * tiles * HALO * width, (3 * depth + depth // 2) * HALO
    total = jnp.zeros((levels * rows, columns), jnp.float32)
    for index in range(9):
        which, oy = index // 3, index % 3 - 1
        oz = (step, 0, -step)[which]
        if oy == 0:
            source, at = (near, own, far)[which], level_at
        else:
            source, at = (fleft, None, fright)[oy + 1], window_at + which * LISTED
        one, two = [], []
        for k in range(LISTED):
            cell = source[pl.ds(at + k, 1), :].astype(jnp.int32)
            x = cell % columns
            y = cell // columns % width + oy * width + RING
            z = cell // (columns * width) + oz * depth + RING
            fits = (cell >= 0) & (y >= 0) & (y < rows) & (z >= 0) & (z < levels)
            row = jnp.where(fits, z * rows + y % 3 * 8 + y // 3, -1)
            if which != 1:
                other = place_z + oz
                row = jnp.where((other >= 0) & (other < count_z), row, -1)
            one.append((row_iota == row).astype(jnp.float32).astype(jnp.bfloat16))
            two.append((col_iota == x).astype(jnp.float32).astype(jnp.bfloat16))
        total = total + lax.dot_general(
            jnp.concatenate(one, 1),
            jnp.concatenate(two, 1),
            (((1,), (1,)), ((), ())),
            preferred_element_type=jnp.float32,
        )
    for t in range(tiles):
        out[t] = total[:, t * LANES : (t + 1) * LANES].reshape(levels, rows, LANES)


def xdiff(value, first, last, nleft, nright):
    ahead = pltpu.roll(value, LANES - 1, 2)
    behind = pltpu.roll(value, 1, 2)
    parts = []
    for i in range(value.shape[0]):
        right = jnp.where(last, ahead[nright[i]], ahead[i])
        left = jnp.where(first, behind[nleft[i]], behind[i])
        parts.append(right - left)
    return jnp.stack(parts)


def rows_of(k):
    return pl.ds(8 * k, 8)


def ydiff(ring, count):
    row = lax.broadcasted_iota(jnp.int32, (8, LANES), 0)
    n = len(ring)
    if n == count == 3:
        return [
            ring[1] - pltpu.roll(ring[2], 1, 1),
            ring[2] - ring[0],
            pltpu.roll(ring[0], 7, 1) - ring[1],
        ]
    edge = ring[3]
    parts = [
        ring[1] - pltpu.roll(jnp.where(row == 7, edge, ring[2]), 1, 1),
        ring[2] - ring[0],
        pltpu.roll(jnp.where(row == 0, edge, ring[0]), 7, 1) - ring[1],
    ]
    if count == 4:
        parts.append(
            pltpu.roll(jnp.where(row == 0, ring[0], edge), 7, 1)
            - pltpu.roll(jnp.where(row == 7, ring[2], edge), 1, 1)
        )
    return parts


TAU = ((0, 3, 4), (3, 1, 5), (4, 5, 2))


def tau_level(src, tau, part, z, inner, ring, count, span, seam, inside, outermost):
    first, last, nleft, nright = seam
    u = [[src[c, span, z, rows_of(k), :] for k in range(ring)] for c in range(3)]
    dy = [ydiff(v, count) for v in u]
    for k in range(count):
        here = rows_of(k)
        gx = [xdiff(u[c][k], first, last, nleft, nright) for c in range(3)]
        gy = [dy[c][k] for c in range(3)]
        gz = [src[c, span, z + 1, here, :] - src[c, span, z - 1, here, :] for c in range(3)]
        xy = gx[1] + gy[0]
        xz = gx[2] + gz[0]
        yz = gy[2] + gz[1]
        diag = gx[0] * gx[0] + gy[1] * gy[1] + gz[2] * gz[2]
        off = xy * xy + xz * xz + yz * yz
        visc = jnp.sqrt(0.5 * diag + 0.25 * off)
        if inside is not None:
            visc = visc * inside
        half = visc * 0.5
        parts = ((visc, gx[0]), (visc, gy[1]), (visc, gz[2]), (half, xy), (half, xz), (half, yz))
        edge = k == inner
        for i, (scale, rate) in enumerate(parts):
            if (outermost and i not in TAU[2]) or (edge and i not in TAU[1]):
                continue
            tau[i, span, z, here, :] = scale * rate
        if outermost or edge:
            continue
        scaled = [u[c][k] * (-0.5 * time_step) for c in range(3)]
        for c in range(3):
            part[c, span, z, here, :] = u[c][k] + (
                scaled[0] * gx[c] + scaled[1] * gy[c] + scaled[2] * gz[c]
            )


def out_level(base, tau, part, z, ring, count, span, seam, weights):
    first, last, nleft, nright = seam
    keep, take = weights
    results = [[] for _ in range(count)]
    for c in range(3):
        dy = ydiff([tau[TAU[c][1], span, z, rows_of(k), :] for k in range(ring)], count)
        for k in range(count):
            here = rows_of(k)
            div = xdiff(tau[TAU[c][0], span, z, here, :], first, last, nleft, nright) + dy[k]
            div = div + (
                tau[TAU[c][2], span, z + 1, here, :] - tau[TAU[c][2], span, z - 1, here, :]
            )
            value = part[c, span, z, here, :] * take + div * (take * time_step * 0.5 * smag_coef)
            if keep:
                value = value + keep * base[c, span, z, here, :]
            results[k].append(value)
    return results


def assemble(dims, u, left, right, fringe, fleft, fright, near, far, fnear, ffar, cnear, cfar, u0):
    tiles, depth, width = dims
    table, total = corner_rows()
    half, rows = depth // 2, width + 2 * RING
    own = pl.ds(RING, width)

    def side_rows(dst, side, value):
        n = value.shape[0]
        if side == 1:
            dst[pl.ds(RING + width, n), :] = value
        else:
            keep = min(n, RING)
            dst[pl.ds(RING - keep, keep), :] = value[n - keep :]
            if n > RING:
                dst[pl.ds(rows + 8 - (n - RING), n - RING), :] = value[: n - RING]

    def unpacked(source, at, n, group):
        value = source[pl.ds(at, n), :]
        return pltpu.roll(value, LANES - GROUP * group, 1) if group else value

    for c in range(3):
        for z in range(depth):
            for t in range(tiles):
                dst = u0.at[c, t, z + HALO]
                dst[own, :] = u[c, z, :, pl.ds(t * LANES, LANES)]
                at = pl.ds(((c * tiles + t) * depth + z) * HALO, HALO)
                side_rows(dst, 0, left[at, :])
                side_rows(dst, 1, right[at, :])
            dst = u0.at[c, tiles, z + HALO]
            at = c * depth + z
            dst[own, :] = fringe[pl.ds(at * width, width), :]
            side_rows(dst, 0, fleft[pl.ds(at * HALO, HALO), :])
            side_rows(dst, 1, fright[pl.ds(at * HALO, HALO), :])
            dst = u0.at[c, tiles + 1, z + HALO]
            group, at = c * 2 + z // half, 3 * depth + z % half
            dst[own, :] = unpacked(fringe, at * width, width, group)
            side_rows(dst, 0, unpacked(fleft, at * HALO, HALO, group))
            side_rows(dst, 1, unpacked(fright, at * HALO, HALO, group))

    def vertical(even):
        for over, levels, window, corners in (
            (even, near, fnear, cnear),
            (not even, far, ffar, cfar),
        ):
            for c in range(3):
                for h in range(HALO):
                    z = HALO + depth + h if over else h
                    for t in range(tiles):
                        at = ((c * tiles + t) * HALO + h) * width
                        u0[c, t, z, own, :] = levels[pl.ds(at, width), :]
                    u0[c, tiles, z, own, :] = window[pl.ds((c * HALO + h) * width, width), :]
                    level = h if over else depth - HALO + h
                    at = (3 * HALO + level % half) * width
                    u0[c, tiles + 1, z, own, :] = unpacked(window, at, width, c * 2 + level // half)
                for distance, n, offset in table:
                    z = HALO + depth + distance - 1 if over else HALO - distance
                    for side in range(2):
                        for t in range(tiles + 1):
                            at = (c * tiles + t) if t < tiles else 3 * tiles + c
                            at = (at * 2 + side) * total + offset
                            side_rows(u0.at[c, t, z], side, corners[pl.ds(at, n), :])
                        level = distance - 1 if over else depth - distance
                        at = 3 * (tiles + 1) * 2 * total + (side * half + level % half) * HALO
                        at = at + (HALO - n if side == 0 else 0)
                        value = unpacked(corners, at, n, c * 2 + level // half)
                        side_rows(u0.at[c, tiles + 1, z], side, value)

    parity(vertical)


def step_kernel(
    dims, first_column, u, left, right, fringe, fleft, fright, near, far, fnear, ffar,
    cnear, cfar, count, out, u0, u1, u2, tau, part,
):
    tiles, depth, width = dims
    start = first_column[0]
    _, lane0 = place(start, tiles * LANES)
    main = lax.axis_index("box")
    bottom = (lax.axis_index("gz") == 0).astype(jnp.int32)
    top = (lax.axis_index("gz") == lax.axis_size("gz") - 1).astype(jnp.int32)
    assemble(dims, u, left, right, fringe, fleft, fright, near, far, fnear, ffar, cnear, cfar, u0)

    def clear(z):
        for c in range(3):
            u0[c, :, z] = jnp.zeros(u0.shape[1:2] + u0.shape[3:], jnp.float32)

    @pl.when(bottom == 1)
    def _():
        lax.fori_loop(0, HALO, lambda i, _: clear(i), None)

    @pl.when(top == 1)
    def _():
        lax.fori_loop(0, HALO, lambda i, _: clear(HALO + depth + i), None)

    def interleave(z, carry):
        for c in range(3):
            for t in range(tiles + 2):
                values = [u0[c, t, z, pl.ds(k, 8, stride=3), :] for k in range(3)]
                for k in range(3):
                    u0[c, t, z, rows_of(k), :] = values[k]
        return carry

    lax.fori_loop(0, depth + 2 * HALO, interleave, 0)

    lane = lax.broadcasted_iota(jnp.int32, (8, LANES), 1)
    order = list(range(tiles))
    main_seam = (lane == 0, lane == LANES - 1, order[-1:] + order[:-1], order[1:] + order[:1])
    window_seam = (lane == lane0, lane == lax.rem(lane0 + LANES - 1, LANES), [1, 0], [1, 0])
    main_span, window_span = slice(0, tiles), slice(tiles, tiles + 2)
    inner = (width + 2 * RING) // 8

    def inside_of(z):
        if HALO <= z < HALO + depth:
            return None
        return 1.0 - (bottom if z < HALO else top).astype(jnp.float32)

    def outside(z):
        return max(HALO - z, z - (HALO + depth - 1), 0)

    def stage(src, dst, margin, weights, span, seam, blended):
        low, high = HALO - margin, HALO + depth + margin
        for z in range(low, high):
            reach = margin - outside(z)
            ring = inner + 1 if reach > RING - 1 else inner
            tiles_here = inner + 1 if reach > RING else inner
            tau_level(
                src, tau, part, z, inner, ring, tiles_here, span, seam, inside_of(z), reach == 0
            )
            if z > low + 1:
                new_level(src, dst, margin - 1, weights, span, seam, blended, z - 1)

    def new_level(src, dst, margin, weights, span, seam, blended, z):
        if True:
            ring = inner + 1 if margin - outside(z) >= RING else inner
            level = out_level(u0, tau, part, z, ring, inner, span, seam, weights)
            for k in range(inner):
                here = rows_of(k)
                values = level[k]
                if blended:
                    ux = src[0, span, z, here, :]
                    times = count[:, z - HALO + RING, here, :]
                    factor = jnp.where(main == 1, -drag_coef * time_step * weights[1], 0.0)
                    values[0] = values[0] + (times * factor) * (ux * jnp.abs(ux))
                for c in range(3):
                    value = values[c]
                    if blended:
                        near_part = dst[c, tiles, z, here, :]
                        far_part = dst[c, tiles + 1, z, here, :]
                        parts = []
                        for t in range(tiles):
                            col = lane + t * LANES
                            mask = (col >= start) & (col < start + FW) & (main == 1)
                            other = jnp.where(col < start + LANES - HALO, near_part, far_part)
                            parts.append(jnp.where(mask, 0.5 * (value[t] + other), value[t]))
                        value = jnp.stack(parts)
                    if inside_of(z) is not None:
                        value = value * inside_of(z)
                    dst[c, span, z, here, :] = value

    stages = (
        (u0, u1, HALO - 1, (0.0, 1.0)),
        (u1, u2, HALO - 3, (0.75, 0.25)),
        (u2, u1, HALO - 5, (1.0 / 3.0, 2.0 / 3.0)),
    )
    for src, dst, margin, weights in stages:

        @pl.when(main == 1)
        def _():
            stage(src, dst, margin, weights, window_span, window_seam, False)

        stage(src, dst, margin, weights, main_span, main_seam, True)
    for c in range(3):
        for t in range(tiles):
            for z in range(HALO, HALO + depth):
                for k in range(3):
                    u2[c, t, z, pl.ds(k, 8, stride=3), :] = u1[c, t, z, rows_of(k), :]
                out[c, z - HALO, :, pl.ds(t * LANES, LANES)] = u2[c, t, z, pl.ds(RING, width), :]


def around(axis, by):
    count = lax.axis_size(axis)
    return [(i, (i + by) % count) for i in range(count)]


def swaps(axis, phase):
    count = lax.axis_size(axis)
    partners = [i + 1 if i % 2 == phase else i - 1 for i in range(count)]
    return [(i, p if 0 <= p < count else i) for i, p in enumerate(partners)]


def per_device(velocity, turbine_cells, turbine_count, fringe_start):
    u = velocity[0]
    _, depth, width, columns = u.shape
    tiles = columns // LANES
    dims = (tiles, depth, width)
    half = depth // 2

    def shapes(*rows):
        return [((r + 7) // 8 * 8, LANES) for r in rows]

    window = (3 * depth + half) * width
    halo = 3 * tiles * depth * HALO
    level = 3 * tiles * HALO * width + LISTED
    window_halo = (3 * depth + half) * HALO + 3 * LISTED
    window_level = (3 * HALO + half) * width
    corner = 3 * (tiles + 1) * 2 * corner_rows()[1] + 2 * half * HALO

    fringe, up, down, first, second = call(
        functools.partial(pack_own, dims),
        shapes(window, halo, halo, level, level),
        (fringe_start, turbine_count, turbine_cells, u),
        2,
        12,
        1,
    )
    fringe = lax.ppermute(fringe, "box", [(0, 1), (1, 0)])
    left = lax.ppermute(up, "gy", around("gy", 1))
    right = lax.ppermute(down, "gy", around("gy", -1))
    near = lax.ppermute(first, "gz", swaps("gz", 0))
    far = lax.ppermute(second, "gz", swaps("gz", 1))
    fup, fdown, ffirst, fsecond = call(
        functools.partial(pack_window, dims),
        shapes(window_halo, window_halo, window_level, window_level),
        (first, near, far, fringe),
        0,
        12,
        1,
    )
    fleft = lax.ppermute(fup, "gy", around("gy", 1))
    fright = lax.ppermute(fdown, "gy", around("gy", -1))
    fnear = lax.ppermute(ffirst, "gz", swaps("gz", 0))
    ffar = lax.ppermute(fsecond, "gz", swaps("gz", 1))
    cfirst, csecond = call(
        functools.partial(pack_corners, dims),
        shapes(corner, corner),
        (left, right, fleft, fright, fnear, ffar),
        0,
        10,
        1,
    )
    cfar = lax.ppermute(csecond, "gz", swaps("gz", 1))
    cnear = lax.ppermute(cfirst, "gz", swaps("gz", 0))

    (count,) = call(
        functools.partial(multiplicity, dims),
        [(tiles, depth + 2 * RING, width + 2 * RING, LANES)],
        (first, near, far, fleft, fright),
        0,
        12,
        8_000_000,
    )
    ext = (tiles + 2, depth + 2 * HALO, width + 2 * RING + 8, LANES)
    (out,) = call(
        functools.partial(step_kernel, dims),
        [u.shape],
        (fringe_start, u, left, right, fringe, fleft, fright, near, far, fnear, ffar, cnear, cfar, count),
        1,
        48,
        8_000_000,
        [pltpu.VMEM((n,) + ext, jnp.float32) for n in (3, 3, 3, 6, 3)],
    )
    return out[None]


def solution(mesh):
    placed = (P("box", None, "gz", "gy", None), P("gz", "gy", None), P("gz", "gy"), P())
    return jax.shard_map(
        per_device,
        mesh=mesh,
        in_specs=placed,
        out_specs=P("box", None, "gz", "gy", None),
        check_vma=False,
    )
```

```python
import functools

import jax
import jax.numpy as jnp
from jax import lax
from jax.experimental import pallas as pl
from jax.experimental.pallas import tpu as pltpu
from jax.sharding import PartitionSpec as P

FW = 128
LANES = 128
HALO = 6
RING = HALO - 2
GROUP = 16

smag_coef = 0.1024
drag_coef = 0.665
time_step = 0.2
LISTED = 4


def corner_rows():
    offset, table = 0, []
    for distance in range(1, HALO):
        table.append((distance, HALO - distance, offset))
        offset += HALO - distance
    return table, offset


def whole_vmem(count):
    return [pl.BlockSpec(memory_space=pltpu.VMEM)] * count


def call(kernel, outs, ins, smem, limit, cost, scratch=()):
    specs = [
        pl.BlockSpec(memory_space=pltpu.SMEM if i < smem else pltpu.VMEM) for i in range(len(ins))
    ]
    return pl.pallas_call(
        kernel,
        out_shape=[jax.ShapeDtypeStruct(shape, jnp.float32) for shape in outs],
        in_specs=specs,
        out_specs=whole_vmem(len(outs)),
        scratch_shapes=list(scratch),
        compiler_params=pltpu.CompilerParams(vmem_limit_bytes=limit * 1024 * 1024),
        cost_estimate=pl.CostEstimate(flops=cost, bytes_accessed=cost, transcendentals=0),
    )(*ins)


def place(start, columns):
    origin = lax.rem(start + columns - HALO, columns)
    return origin // LANES, lax.rem(origin, LANES)


def parity(body):
    even = lax.rem(lax.axis_index("gz"), 2) == 0
    pl.when(even)(functools.partial(body, True))
    pl.when(jnp.logical_not(even))(functools.partial(body, False))


def pack_own(dims, start, live, cells, u, fringe, up, down, first, second):
    tiles, depth, width = dims
    tile0, lane0 = place(start[0], tiles * LANES)
    lane = lax.broadcasted_iota(jnp.int32, (width, LANES), 1)
    offset = lax.rem(lane - lane0 + LANES, LANES)
    picked = [
        pl.ds(pl.multiple_of(lax.rem(tile0 + k, tiles) * LANES, LANES), LANES) for k in range(3)
    ]
    slot = lax.broadcasted_iota(jnp.int32, (1, LANES), 1)
    half = depth // 2
    for zz in range(half):
        packed = None
        for c in range(3):
            for part in range(2):
                z = zz + part * half
                rows = [u[c, z, :, p] for p in picked]
                at = (c * depth + z) * width
                fringe[pl.ds(at, width), :] = jnp.where(lane >= lane0, rows[0], rows[1])
                last = jnp.where(lane >= lane0, rows[1], rows[2])
                group = GROUP * (c * 2 + part)
                if packed is None:
                    packed = last
                else:
                    packed = jnp.where(offset >= group, pltpu.roll(last, group, 1), packed)
        fringe[pl.ds((3 * depth + zz) * width, width), :] = packed
    for c in range(3):
        for t in range(tiles):
            cols = pl.ds(t * LANES, LANES)
            for z in range(depth):
                at = ((c * tiles + t) * depth + z) * HALO
                up[pl.ds(at, HALO), :] = u[c, z, width - HALO :, cols]
                down[pl.ds(at, HALO), :] = u[c, z, :HALO, cols]
    for k in range(LISTED):
        row = cells[0, :, pl.ds(k * LANES, LANES)]
        row = jnp.where(slot + k * LANES < live[0, 0], row, -1).astype(jnp.float32)
        for out in (first, second):
            out[pl.ds(3 * tiles * HALO * width + k, 1), :] = row

    def levels(even):
        above, below = (first, second) if even else (second, first)
        for c in range(3):
            for t in range(tiles):
                cols = pl.ds(t * LANES, LANES)
                for h in range(HALO):
                    at = ((c * tiles + t) * HALO + h) * width
                    above[pl.ds(at, width), :] = u[c, depth - HALO + h, :, cols]
                    below[pl.ds(at, width), :] = u[c, h, :, cols]

    parity(levels)


def pack_window(dims, own, near, far, fringe, fup, fdown, first, second):
    tiles, depth, width = dims
    half = depth // 2
    listed, list_at = 3 * tiles * HALO * width, (3 * depth + half) * HALO
    for k, source in enumerate((near, own, far)):
        for out in (fup, fdown):
            out[pl.ds(list_at + k * LISTED, LISTED), :] = source[pl.ds(listed, LISTED), :]
    for at in range(3 * depth + half):
        fup[pl.ds(at * HALO, HALO), :] = fringe[pl.ds(at * width + width - HALO, HALO), :]
        fdown[pl.ds(at * HALO, HALO), :] = fringe[pl.ds(at * width, HALO), :]
    for out in (first, second):
        for zz in range(half):
            out[pl.ds((3 * HALO + zz) * width, width), :] = fringe[
                pl.ds((3 * depth + zz) * width, width), :
            ]

    def levels(even):
        above, below = (first, second) if even else (second, first)
        for c in range(3):
            for h in range(HALO):
                at = pl.ds((c * HALO + h) * width, width)
                above[at, :] = fringe[pl.ds((c * depth + depth - HALO + h) * width, width), :]
                below[at, :] = fringe[pl.ds((c * depth + h) * width, width), :]

    parity(levels)


def pack_corners(dims, left, right, fleft, fright, fnear, ffar, first, second):
    tiles, depth, _ = dims
    table, total = corner_rows()
    half = depth // 2
    tail = 3 * (tiles + 1) * 2 * total
    for out in (first, second):
        for side, source in enumerate((fleft, fright)):
            out[pl.ds(tail + side * half * HALO, half * HALO), :] = source[
                pl.ds(3 * depth * HALO, half * HALO), :
            ]

    def corners(even):
        above, below = (first, second) if even else (second, first)
        for c in range(3):
            for t in range(tiles + 1):
                for side in range(2):
                    for distance, rows, offset in table:
                        if t < tiles:
                            at = (c * tiles + t) * 2 + side
                            source, row = (left, right)[side], (c * tiles + t) * depth
                        else:
                            at = (3 * tiles + c) * 2 + side
                            source, row = (fleft, fright)[side], c * depth
                        skip = HALO - rows if side == 0 else 0
                        for out, z in ((above, depth - distance), (below, distance - 1)):
                            out[pl.ds(at * total + offset, rows), :] = source[
                                pl.ds((row + z) * HALO + skip, rows), :
                            ]

    parity(corners)


def multiplicity(dims, own, near, far, fleft, fright, out):
    tiles, depth, width = dims
    rows, levels, columns = width + 2 * RING, depth + 2 * RING, tiles * LANES
    place_z, count_z = lax.axis_index("gz"), lax.axis_size("gz")
    step = 1 - 2 * lax.rem(place_z, 2)
    row_iota = lax.broadcasted_iota(jnp.int32, (levels * rows, LANES), 0)
    col_iota = lax.broadcasted_iota(jnp.int32, (columns, LANES), 0)
    level_at, window_at = 3 * tiles * HALO * width, (3 * depth + depth // 2) * HALO
    total = jnp.zeros((levels * rows, columns), jnp.float32)
    for index in range(9):
        which, oy = index // 3, index % 3 - 1
        oz = (step, 0, -step)[which]
        if oy == 0:
            source, at = (near, own, far)[which], level_at
        else:
            source, at = (fleft, None, fright)[oy + 1], window_at + which * LISTED
        one, two = [], []
        for k in range(LISTED):
            cell = source[pl.ds(at + k, 1), :].astype(jnp.int32)
            x = cell % columns
            y = cell // columns % width + oy * width + RING
            z = cell // (columns * width) + oz * depth + RING
            fits = (cell >= 0) & (y >= 0) & (y < rows) & (z >= 0) & (z < levels)
            row = jnp.where(fits, z * rows + y % 3 * 8 + y // 3, -1)
            if which != 1:
                other = place_z + oz
                row = jnp.where((other >= 0) & (other < count_z), row, -1)
            one.append((row_iota == row).astype(jnp.float32).astype(jnp.bfloat16))
            two.append((col_iota == x).astype(jnp.float32).astype(jnp.bfloat16))
        total = total + lax.dot_general(
            jnp.concatenate(one, 1),
            jnp.concatenate(two, 1),
            (((1,), (1,)), ((), ())),
            preferred_element_type=jnp.float32,
        )
    for t in range(tiles):
        out[t] = total[:, t * LANES : (t + 1) * LANES].reshape(levels, rows, LANES)


def xdiff(value, first, last, nleft, nright):
    ahead = pltpu.roll(value, LANES - 1, 2)
    behind = pltpu.roll(value, 1, 2)
    parts = []
    for i in range(value.shape[0]):
        right = jnp.where(last, ahead[nright[i]], ahead[i])
        left = jnp.where(first, behind[nleft[i]], behind[i])
        parts.append(right - left)
    return jnp.stack(parts)


def rows_of(k):
    return pl.ds(8 * k, 8)


def ydiff(ring, count):
    row = lax.broadcasted_iota(jnp.int32, (8, LANES), 0)
    n = len(ring)
    if n == count == 3:
        return [
            ring[1] - pltpu.roll(ring[2], 1, 1),
            ring[2] - ring[0],
            pltpu.roll(ring[0], 7, 1) - ring[1],
        ]
    edge = ring[3]
    parts = [
        ring[1] - pltpu.roll(jnp.where(row == 7, edge, ring[2]), 1, 1),
        ring[2] - ring[0],
        pltpu.roll(jnp.where(row == 0, edge, ring[0]), 7, 1) - ring[1],
    ]
    if count == 4:
        parts.append(
            pltpu.roll(jnp.where(row == 0, ring[0], edge), 7, 1)
            - pltpu.roll(jnp.where(row == 7, ring[2], edge), 1, 1)
        )
    return parts


TAU = ((0, 3, 4), (3, 1, 5), (4, 5, 2))


def tau_level(src, tau, part, z, inner, ring, count, span, seam, inside, outermost):
    first, last, nleft, nright = seam
    u = [[src(z)[c, span, z, rows_of(k), :] for k in range(ring)] for c in range(3)]
    dy = [ydiff(v, count) for v in u]
    for k in range(count):
        here = rows_of(k)
        gx = [xdiff(u[c][k], first, last, nleft, nright) for c in range(3)]
        gy = [dy[c][k] for c in range(3)]
        gz = [src(z + 1)[c, span, z + 1, here, :] - src(z - 1)[c, span, z - 1, here, :] for c in range(3)]
        xy = gx[1] + gy[0]
        xz = gx[2] + gz[0]
        yz = gy[2] + gz[1]
        diag = gx[0] * gx[0] + gy[1] * gy[1] + gz[2] * gz[2]
        off = xy * xy + xz * xz + yz * yz
        visc = jnp.sqrt(0.5 * diag + 0.25 * off)
        if inside is not None:
            visc = visc * inside
        half = visc * 0.5
        parts = ((visc, gx[0]), (visc, gy[1]), (visc, gz[2]), (half, xy), (half, xz), (half, yz))
        edge = k == inner
        for i, (scale, rate) in enumerate(parts):
            if (outermost and i not in TAU[2]) or (edge and i not in TAU[1]):
                continue
            tau[i, span, z, here, :] = scale * rate
        if outermost or edge:
            continue
        scaled = [u[c][k] * (-0.5 * time_step) for c in range(3)]
        for c in range(3):
            part[c, span, z, here, :] = u[c][k] + (
                scaled[0] * gx[c] + scaled[1] * gy[c] + scaled[2] * gz[c]
            )


def out_level(base, tau, part, z, ring, count, span, seam, weights):
    first, last, nleft, nright = seam
    keep, take = weights
    results = [[] for _ in range(count)]
    for c in range(3):
        dy = ydiff([tau[TAU[c][1], span, z, rows_of(k), :] for k in range(ring)], count)
        for k in range(count):
            here = rows_of(k)
            div = xdiff(tau[TAU[c][0], span, z, here, :], first, last, nleft, nright) + dy[k]
            div = div + (
                tau[TAU[c][2], span, z + 1, here, :] - tau[TAU[c][2], span, z - 1, here, :]
            )
            value = part[c, span, z, here, :] * take + div * (take * time_step * 0.5 * smag_coef)
            if keep:
                value = value + keep * base(z)[c, span, z, here, :]
            results[k].append(value)
    return results


def side_rows(width, dst, side, value):
    n = value.shape[0]
    if side == 1:
        dst[pl.ds(RING + width, n), :] = value
    else:
        keep = min(n, RING)
        dst[pl.ds(RING - keep, keep), :] = value[n - keep :]
        if n > RING:
            dst[pl.ds(width + 2 * RING + 8 - (n - RING), n - RING), :] = value[: n - RING]


def unpacked(source, at, n, group):
    value = source[pl.ds(at, n), :]
    return pltpu.roll(value, LANES - GROUP * group, 1) if group else value


def interleave(u0, levels):
    def step(i, carry):
        z = levels(i)
        for c in range(3):
            for t in range(u0.shape[1]):
                values = [u0[c, t, z, pl.ds(k, 8, stride=3), :] for k in range(3)]
                for k in range(3):
                    u0[c, t, z, rows_of(k), :] = values[k]
        return carry

    return step


def assemble(dims, u, left, right, fringe, fleft, fright, near, far, fnear, ffar, u0):
    tiles, depth, width = dims
    half = depth // 2
    own = pl.ds(RING, width)

    for c in range(3):
        for z in range(depth):
            for t in range(tiles):
                dst = u0.at[c, t, z + HALO]
                dst[own, :] = u[c, z, :, pl.ds(t * LANES, LANES)]
                at = pl.ds(((c * tiles + t) * depth + z) * HALO, HALO)
                side_rows(width, dst, 0, left[at, :])
                side_rows(width, dst, 1, right[at, :])
            dst = u0.at[c, tiles, z + HALO]
            at = c * depth + z
            dst[own, :] = fringe[pl.ds(at * width, width), :]
            side_rows(width, dst, 0, fleft[pl.ds(at * HALO, HALO), :])
            side_rows(width, dst, 1, fright[pl.ds(at * HALO, HALO), :])
            dst = u0.at[c, tiles + 1, z + HALO]
            group, at = c * 2 + z // half, 3 * depth + z % half
            dst[own, :] = unpacked(fringe, at * width, width, group)
            side_rows(width, dst, 0, unpacked(fleft, at * HALO, HALO, group))
            side_rows(width, dst, 1, unpacked(fright, at * HALO, HALO, group))

    def vertical(even):
        for over, levels, window in ((even, near, fnear), (not even, far, ffar)):
            for c in range(3):
                for h in range(HALO):
                    z = HALO + depth + h if over else h
                    for t in range(tiles):
                        at = ((c * tiles + t) * HALO + h) * width
                        u0[c, t, z, own, :] = levels[pl.ds(at, width), :]
                    u0[c, tiles, z, own, :] = window[pl.ds((c * HALO + h) * width, width), :]
                    level = h if over else depth - HALO + h
                    at = (3 * HALO + level % half) * width
                    u0[c, tiles + 1, z, own, :] = unpacked(window, at, width, c * 2 + level // half)

    parity(vertical)
    step = interleave(u0, lambda i: jnp.where(i < depth, HALO + i, (i - depth) * (depth + 2 * HALO - 1)))
    lax.fori_loop(0, depth + 2, step, 0)


def corner_levels(depth):
    return list(range(1, HALO)) + list(range(HALO + depth, 2 * HALO + depth - 1))


def add_corners(dims, cnear, cfar, given, u0):
    tiles, depth, width = dims
    table, total = corner_rows()
    half = depth // 2
    for z in corner_levels(depth):
        for c in range(3):
            u0[c, :, z] = given[c, :, z]

    def vertical(even):
        for over, corners in ((even, cnear), (not even, cfar)):
            for c in range(3):
                for distance, n, offset in table:
                    z = HALO + depth + distance - 1 if over else HALO - distance
                    for side in range(2):
                        for t in range(tiles + 1):
                            at = (c * tiles + t) if t < tiles else 3 * tiles + c
                            at = (at * 2 + side) * total + offset
                            side_rows(width, u0.at[c, t, z], side, corners[pl.ds(at, n), :])
                        level = distance - 1 if over else depth - distance
                        at = 3 * (tiles + 1) * 2 * total + (side * half + level % half) * HALO
                        at = at + (HALO - n if side == 0 else 0)
                        value = unpacked(corners, at, n, c * 2 + level // half)
                        side_rows(width, u0.at[c, tiles + 1, z], side, value)

    parity(vertical)
    step = interleave(u0, lambda i: jnp.where(i < HALO - 1, 1 + i, depth + 1 + i))
    lax.fori_loop(0, 2 * (HALO - 1), step, 0)


def step_kernel(dims, first_column, cfar, cnear, count, given, out, u0, u1, u2, tau, part):
    tiles, depth, width = dims
    start = first_column[0]
    _, lane0 = place(start, tiles * LANES)
    main = lax.axis_index("box")
    bottom = (lax.axis_index("gz") == 0).astype(jnp.int32)
    top = (lax.axis_index("gz") == lax.axis_size("gz") - 1).astype(jnp.int32)
    add_corners(dims, cnear, cfar, given, u0)

    def clear(z):
        for c in range(3):
            u0[c, :, z] = jnp.zeros(u0.shape[1:2] + u0.shape[3:], jnp.float32)

    @pl.when(bottom == 1)
    def _():
        lax.fori_loop(1, HALO, lambda i, _: clear(i), None)

    @pl.when(top == 1)
    def _():
        lax.fori_loop(0, HALO - 1, lambda i, _: clear(HALO + depth + i), None)

    lane = lax.broadcasted_iota(jnp.int32, (8, LANES), 1)
    order = list(range(tiles))
    main_seam = (lane == 0, lane == LANES - 1, order[-1:] + order[:-1], order[1:] + order[:1])
    window_seam = (lane == lane0, lane == lax.rem(lane0 + LANES - 1, LANES), [1, 0], [1, 0])
    main_span, window_span = slice(0, tiles), slice(tiles, tiles + 2)
    inner = (width + 2 * RING) // 8
    touched = corner_levels(depth)

    def first_field(z):
        return u0 if z in touched else given

    def inside_of(z):
        if HALO <= z < HALO + depth:
            return None
        return 1.0 - (bottom if z < HALO else top).astype(jnp.float32)

    def outside(z):
        return max(HALO - z, z - (HALO + depth - 1), 0)

    def stage(src, dst, margin, weights, span, seam, blended):
        low, high = HALO - margin, HALO + depth + margin
        for z in range(low, high):
            reach = margin - outside(z)
            ring = inner + 1 if reach > RING - 1 else inner
            tiles_here = inner + 1 if reach > RING else inner
            tau_level(
                src, tau, part, z, inner, ring, tiles_here, span, seam, inside_of(z), reach == 0
            )
            if z > low + 1:
                new_level(src, dst, margin - 1, weights, span, seam, blended, z - 1)

    def new_level(src, dst, margin, weights, span, seam, blended, z):
        if True:
            ring = inner + 1 if margin - outside(z) >= RING else inner
            level = out_level(first_field, tau, part, z, ring, inner, span, seam, weights)
            for k in range(inner):
                here = rows_of(k)
                values = level[k]
                if blended:
                    ux = src(z)[0, span, z, here, :]
                    times = count[:, z - HALO + RING, here, :]
                    factor = jnp.where(main == 1, -drag_coef * time_step * weights[1], 0.0)
                    values[0] = values[0] + (times * factor) * (ux * jnp.abs(ux))
                for c in range(3):
                    value = values[c]
                    if blended:
                        near_part = dst[c, tiles, z, here, :]
                        far_part = dst[c, tiles + 1, z, here, :]
                        parts = []
                        for t in range(tiles):
                            col = lane + t * LANES
                            mask = (col >= start) & (col < start + FW) & (main == 1)
                            other = jnp.where(col < start + LANES - HALO, near_part, far_part)
                            parts.append(jnp.where(mask, 0.5 * (value[t] + other), value[t]))
                        value = jnp.stack(parts)
                    if inside_of(z) is not None:
                        value = value * inside_of(z)
                    dst[c, span, z, here, :] = value

    stages = (
        (first_field, u1, HALO - 1, (0.0, 1.0)),
        (lambda z: u1, u2, HALO - 3, (0.75, 0.25)),
        (lambda z: u2, u1, HALO - 5, (1.0 / 3.0, 2.0 / 3.0)),
    )
    for src, dst, margin, weights in stages:

        @pl.when(main == 1)
        def _():
            stage(src, dst, margin, weights, window_span, window_seam, False)

        stage(src, dst, margin, weights, main_span, main_seam, True)
    for c in range(3):
        for t in range(tiles):
            for z in range(HALO, HALO + depth):
                for k in range(3):
                    u2[c, t, z, pl.ds(k, 8, stride=3), :] = u1[c, t, z, rows_of(k), :]
                out[c, z - HALO, :, pl.ds(t * LANES, LANES)] = u2[c, t, z, pl.ds(RING, width), :]


def around(axis, by):
    count = lax.axis_size(axis)
    return [(i, (i + by) % count) for i in range(count)]


def swaps(axis, phase):
    count = lax.axis_size(axis)
    partners = [i + 1 if i % 2 == phase else i - 1 for i in range(count)]
    return [(i, p if 0 <= p < count else i) for i, p in enumerate(partners)]


def per_device(velocity, turbine_cells, turbine_count, fringe_start):
    u = velocity[0]
    _, depth, width, columns = u.shape
    tiles = columns // LANES
    dims = (tiles, depth, width)
    half = depth // 2

    def shapes(*rows):
        return [((r + 7) // 8 * 8, LANES) for r in rows]

    window = (3 * depth + half) * width
    halo = 3 * tiles * depth * HALO
    level = 3 * tiles * HALO * width + LISTED
    window_halo = (3 * depth + half) * HALO + 3 * LISTED
    window_level = (3 * HALO + half) * width
    corner = 3 * (tiles + 1) * 2 * corner_rows()[1] + 2 * half * HALO

    fringe, up, down, first, second = call(
        functools.partial(pack_own, dims),
        shapes(window, halo, halo, level, level),
        (fringe_start, turbine_count, turbine_cells, u),
        2,
        12,
        1,
    )
    fringe = lax.ppermute(fringe, "box", [(0, 1), (1, 0)])
    left = lax.ppermute(up, "gy", around("gy", 1))
    right = lax.ppermute(down, "gy", around("gy", -1))
    near = lax.ppermute(first, "gz", swaps("gz", 0))
    far = lax.ppermute(second, "gz", swaps("gz", 1))
    fup, fdown, ffirst, fsecond = call(
        functools.partial(pack_window, dims),
        shapes(window_halo, window_halo, window_level, window_level),
        (first, near, far, fringe),
        0,
        12,
        1,
    )
    fleft = lax.ppermute(fup, "gy", around("gy", 1))
    fright = lax.ppermute(fdown, "gy", around("gy", -1))
    fnear = lax.ppermute(ffirst, "gz", swaps("gz", 0))
    ffar = lax.ppermute(fsecond, "gz", swaps("gz", 1))
    cfirst, csecond = call(
        functools.partial(pack_corners, dims),
        shapes(corner, corner),
        (left, right, fleft, fright, fnear, ffar),
        0,
        10,
        1,
    )
    cfar = lax.ppermute(csecond, "gz", swaps("gz", 1))
    cnear = lax.ppermute(cfirst, "gz", swaps("gz", 0))

    (count,) = call(
        functools.partial(multiplicity, dims),
        [(tiles, depth + 2 * RING, width + 2 * RING, LANES)],
        (first, near, far, fleft, fright),
        0,
        12,
        8_000_000,
    )
    ext = (tiles + 2, depth + 2 * HALO, width + 2 * RING + 8, LANES)
    (given,) = call(
        functools.partial(assemble, dims),
        [(3,) + ext],
        (u, left, right, fringe, fleft, fright, near, far, fnear, ffar),
        0,
        16,
        8_000_000,
    )
    (out,) = call(
        functools.partial(step_kernel, dims),
        [u.shape],
        (fringe_start, cfar, cnear, count, given),
        1,
        46,
        8_000_000,
        [pltpu.VMEM((n,) + ext, jnp.float32) for n in (3, 3, 3, 6, 3)],
    )
    return out[None]


def solution(mesh):
    placed = (P("box", None, "gz", "gy", None), P("gz", "gy", None), P("gz", "gy"), P())
    return jax.shard_map(
        per_device,
        mesh=mesh,
        in_specs=placed,
        out_specs=P("box", None, "gz", "gy", None),
        check_vma=False,
    )
```

```python
import functools

import jax
import jax.numpy as jnp
from jax import lax
from jax.experimental import pallas as pl
from jax.experimental.pallas import tpu as pltpu
from jax.sharding import PartitionSpec as P

FW = 128
LANES = 128
HALO = 6
RING = HALO - 2
GROUP = 16

smag_coef = 0.1024
drag_coef = 0.665
time_step = 0.2
LISTED = 4


def corner_rows():
    offset, table = 0, []
    for distance in range(1, HALO):
        table.append((distance, HALO - distance, offset))
        offset += HALO - distance
    return table, offset


def whole_vmem(count):
    return [pl.BlockSpec(memory_space=pltpu.VMEM)] * count


def call(kernel, outs, ins, smem, limit, cost, scratch=()):
    specs = [
        pl.BlockSpec(memory_space=pltpu.SMEM if i < smem else pltpu.VMEM) for i in range(len(ins))
    ]
    return pl.pallas_call(
        kernel,
        out_shape=[jax.ShapeDtypeStruct(shape, jnp.float32) for shape in outs],
        in_specs=specs,
        out_specs=whole_vmem(len(outs)),
        scratch_shapes=list(scratch),
        compiler_params=pltpu.CompilerParams(vmem_limit_bytes=limit * 1024 * 1024),
        cost_estimate=pl.CostEstimate(flops=cost, bytes_accessed=cost, transcendentals=0),
    )(*ins)


def place(start, columns):
    origin = lax.rem(start + columns - HALO, columns)
    return origin // LANES, lax.rem(origin, LANES)


def parity(body):
    even = lax.rem(lax.axis_index("gz"), 2) == 0
    pl.when(even)(functools.partial(body, True))
    pl.when(jnp.logical_not(even))(functools.partial(body, False))


def pack_own(dims, start, live, cells, u, fringe, up, down, first, second):
    tiles, depth, width = dims
    tile0, lane0 = place(start[0], tiles * LANES)
    lane = lax.broadcasted_iota(jnp.int32, (width, LANES), 1)
    offset = lax.rem(lane - lane0 + LANES, LANES)
    picked = [
        pl.ds(pl.multiple_of(lax.rem(tile0 + k, tiles) * LANES, LANES), LANES) for k in range(3)
    ]
    slot = lax.broadcasted_iota(jnp.int32, (1, LANES), 1)
    half = depth // 2
    for zz in range(half):
        packed = None
        for c in range(3):
            for part in range(2):
                z = zz + part * half
                rows = [u[c, z, :, p] for p in picked]
                at = (c * depth + z) * width
                fringe[pl.ds(at, width), :] = jnp.where(lane >= lane0, rows[0], rows[1])
                last = jnp.where(lane >= lane0, rows[1], rows[2])
                group = GROUP * (c * 2 + part)
                if packed is None:
                    packed = last
                else:
                    packed = jnp.where(offset >= group, pltpu.roll(last, group, 1), packed)
        fringe[pl.ds((3 * depth + zz) * width, width), :] = packed
    for c in range(3):
        for t in range(tiles):
            cols = pl.ds(t * LANES, LANES)
            for z in range(depth):
                at = ((c * tiles + t) * depth + z) * HALO
                up[pl.ds(at, HALO), :] = u[c, z, width - HALO :, cols]
                down[pl.ds(at, HALO), :] = u[c, z, :HALO, cols]
    for k in range(LISTED):
        row = cells[0, :, pl.ds(k * LANES, LANES)]
        row = jnp.where(slot + k * LANES < live[0, 0], row, -1).astype(jnp.float32)
        for out in (first, second):
            out[pl.ds(3 * tiles * HALO * width + k, 1), :] = row

    def levels(even):
        above, below = (first, second) if even else (second, first)
        for c in range(3):
            for t in range(tiles):
                cols = pl.ds(t * LANES, LANES)
                for h in range(HALO):
                    at = ((c * tiles + t) * HALO + h) * width
                    above[pl.ds(at, width), :] = u[c, depth - HALO + h, :, cols]
                    below[pl.ds(at, width), :] = u[c, h, :, cols]

    parity(levels)


def pack_window_rows(dims, own, near, far, fringe, fup, fdown):
    tiles, depth, width = dims
    half = depth // 2
    listed, list_at = 3 * tiles * HALO * width, (3 * depth + half) * HALO
    for k, source in enumerate((near, own, far)):
        for out in (fup, fdown):
            out[pl.ds(list_at + k * LISTED, LISTED), :] = source[pl.ds(listed, LISTED), :]
    for at in range(3 * depth + half):
        fup[pl.ds(at * HALO, HALO), :] = fringe[pl.ds(at * width + width - HALO, HALO), :]
        fdown[pl.ds(at * HALO, HALO), :] = fringe[pl.ds(at * width, HALO), :]


def pack_window_levels(dims, fringe, first, second):
    tiles, depth, width = dims
    half = depth // 2
    for out in (first, second):
        for zz in range(half):
            out[pl.ds((3 * HALO + zz) * width, width), :] = fringe[
                pl.ds((3 * depth + zz) * width, width), :
            ]

    def levels(even):
        above, below = (first, second) if even else (second, first)
        for c in range(3):
            for h in range(HALO):
                at = pl.ds((c * HALO + h) * width, width)
                above[at, :] = fringe[pl.ds((c * depth + depth - HALO + h) * width, width), :]
                below[at, :] = fringe[pl.ds((c * depth + h) * width, width), :]

    parity(levels)


def pack_corners(dims, left, right, fleft, fright, fnear, ffar, first, second):
    tiles, depth, _ = dims
    table, total = corner_rows()
    half = depth // 2
    tail = 3 * (tiles + 1) * 2 * total
    for out in (first, second):
        for side, source in enumerate((fleft, fright)):
            out[pl.ds(tail + side * half * HALO, half * HALO), :] = source[
                pl.ds(3 * depth * HALO, half * HALO), :
            ]

    def corners(even):
        above, below = (first, second) if even else (second, first)
        for c in range(3):
            for t in range(tiles + 1):
                for side in range(2):
                    for distance, rows, offset in table:
                        if t < tiles:
                            at = (c * tiles + t) * 2 + side
                            source, row = (left, right)[side], (c * tiles + t) * depth
                        else:
                            at = (3 * tiles + c) * 2 + side
                            source, row = (fleft, fright)[side], c * depth
                        skip = HALO - rows if side == 0 else 0
                        for out, z in ((above, depth - distance), (below, distance - 1)):
                            out[pl.ds(at * total + offset, rows), :] = source[
                                pl.ds((row + z) * HALO + skip, rows), :
                            ]

    parity(corners)


def multiplicity(dims, own, near, far, fleft, fright, out):
    tiles, depth, width = dims
    rows, levels, columns = width + 2 * RING, depth + 2 * RING, tiles * LANES
    place_z, count_z = lax.axis_index("gz"), lax.axis_size("gz")
    step = 1 - 2 * lax.rem(place_z, 2)
    row_iota = lax.broadcasted_iota(jnp.int32, (levels * rows, LANES), 0)
    col_iota = lax.broadcasted_iota(jnp.int32, (columns, LANES), 0)
    level_at, window_at = 3 * tiles * HALO * width, (3 * depth + depth // 2) * HALO
    total = jnp.zeros((levels * rows, columns), jnp.float32)
    for index in range(9):
        which, oy = index // 3, index % 3 - 1
        oz = (step, 0, -step)[which]
        if oy == 0:
            source, at = (near, own, far)[which], level_at
        else:
            source, at = (fleft, None, fright)[oy + 1], window_at + which * LISTED
        one, two = [], []
        for k in range(LISTED):
            cell = source[pl.ds(at + k, 1), :].astype(jnp.int32)
            x = cell % columns
            y = cell // columns % width + oy * width + RING
            z = cell // (columns * width) + oz * depth + RING
            fits = (cell >= 0) & (y >= 0) & (y < rows) & (z >= 0) & (z < levels)
            row = jnp.where(fits, z * rows + y % 3 * 8 + y // 3, -1)
            if which != 1:
                other = place_z + oz
                row = jnp.where((other >= 0) & (other < count_z), row, -1)
            one.append((row_iota == row).astype(jnp.float32).astype(jnp.bfloat16))
            two.append((col_iota == x).astype(jnp.float32).astype(jnp.bfloat16))
        total = total + lax.dot_general(
            jnp.concatenate(one, 1),
            jnp.concatenate(two, 1),
            (((1,), (1,)), ((), ())),
            preferred_element_type=jnp.float32,
        )
    for t in range(tiles):
        out[t] = total[:, t * LANES : (t + 1) * LANES].reshape(levels, rows, LANES)


def xdiff(value, first, last, nleft, nright):
    ahead = pltpu.roll(value, LANES - 1, 2)
    behind = pltpu.roll(value, 1, 2)
    parts = []
    for i in range(value.shape[0]):
        right = jnp.where(last, ahead[nright[i]], ahead[i])
        left = jnp.where(first, behind[nleft[i]], behind[i])
        parts.append(right - left)
    return jnp.stack(parts)


def rows_of(k):
    return pl.ds(8 * k, 8)


def ydiff(ring, count):
    row = lax.broadcasted_iota(jnp.int32, (8, LANES), 0)
    n = len(ring)
    if n == count == 3:
        return [
            ring[1] - pltpu.roll(ring[2], 1, 1),
            ring[2] - ring[0],
            pltpu.roll(ring[0], 7, 1) - ring[1],
        ]
    edge = ring[3]
    parts = [
        ring[1] - pltpu.roll(jnp.where(row == 7, edge, ring[2]), 1, 1),
        ring[2] - ring[0],
        pltpu.roll(jnp.where(row == 0, edge, ring[0]), 7, 1) - ring[1],
    ]
    if count == 4:
        parts.append(
            pltpu.roll(jnp.where(row == 0, ring[0], edge), 7, 1)
            - pltpu.roll(jnp.where(row == 7, ring[2], edge), 1, 1)
        )
    return parts


TAU = ((0, 3, 4), (3, 1, 5), (4, 5, 2))


def tau_level(src, tau, part, z, inner, ring, count, span, seam, inside, outermost):
    first, last, nleft, nright = seam
    u = [[src(z)[c, span, z, rows_of(k), :] for k in range(ring)] for c in range(3)]
    dy = [ydiff(v, count) for v in u]
    for k in range(count):
        here = rows_of(k)
        gx = [xdiff(u[c][k], first, last, nleft, nright) for c in range(3)]
        gy = [dy[c][k] for c in range(3)]
        gz = [src(z + 1)[c, span, z + 1, here, :] - src(z - 1)[c, span, z - 1, here, :] for c in range(3)]
        xy = gx[1] + gy[0]
        xz = gx[2] + gz[0]
        yz = gy[2] + gz[1]
        diag = gx[0] * gx[0] + gy[1] * gy[1] + gz[2] * gz[2]
        off = xy * xy + xz * xz + yz * yz
        visc = jnp.sqrt(0.5 * diag + 0.25 * off)
        if inside is not None:
            visc = visc * inside
        half = visc * 0.5
        parts = ((visc, gx[0]), (visc, gy[1]), (visc, gz[2]), (half, xy), (half, xz), (half, yz))
        edge = k == inner
        for i, (scale, rate) in enumerate(parts):
            if (outermost and i not in TAU[2]) or (edge and i not in TAU[1]):
                continue
            tau[i, span, z, here, :] = scale * rate
        if outermost or edge:
            continue
        scaled = [u[c][k] * (-0.5 * time_step) for c in range(3)]
        for c in range(3):
            part[c, span, z, here, :] = u[c][k] + (
                scaled[0] * gx[c] + scaled[1] * gy[c] + scaled[2] * gz[c]
            )


def out_level(base, tau, part, z, ring, count, span, seam, weights):
    first, last, nleft, nright = seam
    keep, take = weights
    results = [[] for _ in range(count)]
    for c in range(3):
        dy = ydiff([tau[TAU[c][1], span, z, rows_of(k), :] for k in range(ring)], count)
        for k in range(count):
            here = rows_of(k)
            div = xdiff(tau[TAU[c][0], span, z, here, :], first, last, nleft, nright) + dy[k]
            div = div + (
                tau[TAU[c][2], span, z + 1, here, :] - tau[TAU[c][2], span, z - 1, here, :]
            )
            value = part[c, span, z, here, :] * take + div * (take * time_step * 0.5 * smag_coef)
            if keep:
                value = value + keep * base(z)[c, span, z, here, :]
            results[k].append(value)
    return results


def side_rows(width, dst, side, value):
    n = value.shape[0]
    if side == 1:
        dst[pl.ds(RING + width, n), :] = value
    else:
        keep = min(n, RING)
        dst[pl.ds(RING - keep, keep), :] = value[n - keep :]
        if n > RING:
            dst[pl.ds(width + 2 * RING + 8 - (n - RING), n - RING), :] = value[: n - RING]


def unpacked(source, at, n, group):
    value = source[pl.ds(at, n), :]
    return pltpu.roll(value, LANES - GROUP * group, 1) if group else value


def interleave(u0, levels):
    def step(i, carry):
        z = levels(i)
        for c in range(3):
            for t in range(u0.shape[1]):
                values = [u0[c, t, z, pl.ds(k, 8, stride=3), :] for k in range(3)]
                for k in range(3):
                    u0[c, t, z, rows_of(k), :] = values[k]
        return carry

    return step


def assemble(dims, u, left, right, fringe, fleft, fright, near, far, fnear, ffar, u0):
    tiles, depth, width = dims
    half = depth // 2
    own = pl.ds(RING, width)

    for c in range(3):
        for z in range(depth):
            for t in range(tiles):
                dst = u0.at[c, t, z + HALO]
                dst[own, :] = u[c, z, :, pl.ds(t * LANES, LANES)]
                at = pl.ds(((c * tiles + t) * depth + z) * HALO, HALO)
                side_rows(width, dst, 0, left[at, :])
                side_rows(width, dst, 1, right[at, :])
            dst = u0.at[c, tiles, z + HALO]
            at = c * depth + z
            dst[own, :] = fringe[pl.ds(at * width, width), :]
            side_rows(width, dst, 0, fleft[pl.ds(at * HALO, HALO), :])
            side_rows(width, dst, 1, fright[pl.ds(at * HALO, HALO), :])
            dst = u0.at[c, tiles + 1, z + HALO]
            group, at = c * 2 + z // half, 3 * depth + z % half
            dst[own, :] = unpacked(fringe, at * width, width, group)
            side_rows(width, dst, 0, unpacked(fleft, at * HALO, HALO, group))
            side_rows(width, dst, 1, unpacked(fright, at * HALO, HALO, group))

    def vertical(even):
        for over, levels, window in ((even, near, fnear), (not even, far, ffar)):
            for c in range(3):
                for h in range(HALO):
                    z = HALO + depth + h if over else h
                    for t in range(tiles):
                        at = ((c * tiles + t) * HALO + h) * width
                        u0[c, t, z, own, :] = levels[pl.ds(at, width), :]
                    u0[c, tiles, z, own, :] = window[pl.ds((c * HALO + h) * width, width), :]
                    level = h if over else depth - HALO + h
                    at = (3 * HALO + level % half) * width
                    u0[c, tiles + 1, z, own, :] = unpacked(window, at, width, c * 2 + level // half)

    parity(vertical)
    step = interleave(u0, lambda i: jnp.where(i < depth, HALO + i, (i - depth) * (depth + 2 * HALO - 1)))
    lax.fori_loop(0, depth + 2, step, 0)


def corner_levels(depth):
    return list(range(1, HALO)) + list(range(HALO + depth, 2 * HALO + depth - 1))


def add_corners(dims, cnear, cfar, given, u0):
    tiles, depth, width = dims
    table, total = corner_rows()
    half = depth // 2
    for z in corner_levels(depth):
        for c in range(3):
            u0[c, :, z] = given[c, :, z]

    def vertical(even):
        for over, corners in ((even, cnear), (not even, cfar)):
            for c in range(3):
                for distance, n, offset in table:
                    z = HALO + depth + distance - 1 if over else HALO - distance
                    for side in range(2):
                        for t in range(tiles + 1):
                            at = (c * tiles + t) if t < tiles else 3 * tiles + c
                            at = (at * 2 + side) * total + offset
                            side_rows(width, u0.at[c, t, z], side, corners[pl.ds(at, n), :])
                        level = distance - 1 if over else depth - distance
                        at = 3 * (tiles + 1) * 2 * total + (side * half + level % half) * HALO
                        at = at + (HALO - n if side == 0 else 0)
                        value = unpacked(corners, at, n, c * 2 + level // half)
                        side_rows(width, u0.at[c, tiles + 1, z], side, value)

    parity(vertical)
    step = interleave(u0, lambda i: jnp.where(i < HALO - 1, 1 + i, depth + 1 + i))
    lax.fori_loop(0, 2 * (HALO - 1), step, 0)


def step_kernel(dims, first_column, cfar, cnear, count, given, out, u0, u1, u2, tau, part):
    tiles, depth, width = dims
    start = first_column[0]
    _, lane0 = place(start, tiles * LANES)
    main = lax.axis_index("box")
    bottom = (lax.axis_index("gz") == 0).astype(jnp.int32)
    top = (lax.axis_index("gz") == lax.axis_size("gz") - 1).astype(jnp.int32)
    add_corners(dims, cnear, cfar, given, u0)

    def clear(z):
        for c in range(3):
            u0[c, :, z] = jnp.zeros(u0.shape[1:2] + u0.shape[3:], jnp.float32)

    @pl.when(bottom == 1)
    def _():
        lax.fori_loop(1, HALO, lambda i, _: clear(i), None)

    @pl.when(top == 1)
    def _():
        lax.fori_loop(0, HALO - 1, lambda i, _: clear(HALO + depth + i), None)

    lane = lax.broadcasted_iota(jnp.int32, (8, LANES), 1)
    order = list(range(tiles))
    main_seam = (lane == 0, lane == LANES - 1, order[-1:] + order[:-1], order[1:] + order[:1])
    window_seam = (lane == lane0, lane == lax.rem(lane0 + LANES - 1, LANES), [1, 0], [1, 0])
    main_span, window_span = slice(0, tiles), slice(tiles, tiles + 2)
    inner = (width + 2 * RING) // 8
    touched = corner_levels(depth)

    def first_field(z):
        return u0 if z in touched else given

    def inside_of(z):
        if HALO <= z < HALO + depth:
            return None
        return 1.0 - (bottom if z < HALO else top).astype(jnp.float32)

    def outside(z):
        return max(HALO - z, z - (HALO + depth - 1), 0)

    def stage(src, dst, margin, weights, span, seam, blended):
        low, high = HALO - margin, HALO + depth + margin
        for z in range(low, high):
            reach = margin - outside(z)
            ring = inner + 1 if reach > RING - 1 else inner
            tiles_here = inner + 1 if reach > RING else inner
            tau_level(
                src, tau, part, z, inner, ring, tiles_here, span, seam, inside_of(z), reach == 0
            )
            if z > low + 1:
                new_level(src, dst, margin - 1, weights, span, seam, blended, z - 1)

    def new_level(src, dst, margin, weights, span, seam, blended, z):
        if True:
            ring = inner + 1 if margin - outside(z) >= RING else inner
            level = out_level(first_field, tau, part, z, ring, inner, span, seam, weights)
            for k in range(inner):
                here = rows_of(k)
                values = level[k]
                if blended:
                    ux = src(z)[0, span, z, here, :]
                    times = count[:, z - HALO + RING, here, :]
                    factor = jnp.where(main == 1, -drag_coef * time_step * weights[1], 0.0)
                    values[0] = values[0] + (times * factor) * (ux * jnp.abs(ux))
                for c in range(3):
                    value = values[c]
                    if blended:
                        near_part = dst[c, tiles, z, here, :]
                        far_part = dst[c, tiles + 1, z, here, :]
                        parts = []
                        for t in range(tiles):
                            col = lane + t * LANES
                            mask = (col >= start) & (col < start + FW) & (main == 1)
                            other = jnp.where(col < start + LANES - HALO, near_part, far_part)
                            parts.append(jnp.where(mask, 0.5 * (value[t] + other), value[t]))
                        value = jnp.stack(parts)
                    if inside_of(z) is not None:
                        value = value * inside_of(z)
                    dst[c, span, z, here, :] = value

    stages = (
        (first_field, u1, HALO - 1, (0.0, 1.0)),
        (lambda z: u1, u2, HALO - 3, (0.75, 0.25)),
        (lambda z: u2, u1, HALO - 5, (1.0 / 3.0, 2.0 / 3.0)),
    )
    for src, dst, margin, weights in stages:

        @pl.when(main == 1)
        def _():
            stage(src, dst, margin, weights, window_span, window_seam, False)

        stage(src, dst, margin, weights, main_span, main_seam, True)
    for c in range(3):
        for t in range(tiles):
            for z in range(HALO, HALO + depth):
                for k in range(3):
                    u2[c, t, z, pl.ds(k, 8, stride=3), :] = u1[c, t, z, rows_of(k), :]
                out[c, z - HALO, :, pl.ds(t * LANES, LANES)] = u2[c, t, z, pl.ds(RING, width), :]


def around(axis, by):
    count = lax.axis_size(axis)
    return [(i, (i + by) % count) for i in range(count)]


def swaps(axis, phase):
    count = lax.axis_size(axis)
    partners = [i + 1 if i % 2 == phase else i - 1 for i in range(count)]
    return [(i, p if 0 <= p < count else i) for i, p in enumerate(partners)]


def per_device(velocity, turbine_cells, turbine_count, fringe_start):
    u = velocity[0]
    _, depth, width, columns = u.shape
    tiles = columns // LANES
    dims = (tiles, depth, width)
    half = depth // 2

    def shapes(*rows):
        return [((r + 7) // 8 * 8, LANES) for r in rows]

    window = (3 * depth + half) * width
    halo = 3 * tiles * depth * HALO
    level = 3 * tiles * HALO * width + LISTED
    window_halo = (3 * depth + half) * HALO + 3 * LISTED
    window_level = (3 * HALO + half) * width
    corner = 3 * (tiles + 1) * 2 * corner_rows()[1] + 2 * half * HALO

    fringe, up, down, first, second = call(
        functools.partial(pack_own, dims),
        shapes(window, halo, halo, level, level),
        (fringe_start, turbine_count, turbine_cells, u),
        2,
        12,
        1,
    )
    fringe = lax.ppermute(fringe, "box", [(0, 1), (1, 0)])
    left = lax.ppermute(up, "gy", around("gy", 1))
    right = lax.ppermute(down, "gy", around("gy", -1))
    near = lax.ppermute(first, "gz", swaps("gz", 0))
    far = lax.ppermute(second, "gz", swaps("gz", 1))
    ffirst, fsecond = call(
        functools.partial(pack_window_levels, dims),
        shapes(window_level, window_level),
        (fringe,),
        0,
        12,
        1,
    )
    fup, fdown = call(
        functools.partial(pack_window_rows, dims),
        shapes(window_halo, window_halo),
        (first, near, far, fringe),
        0,
        12,
        1,
    )
    fleft = lax.ppermute(fup, "gy", around("gy", 1))
    fright = lax.ppermute(fdown, "gy", around("gy", -1))
    fnear = lax.ppermute(ffirst, "gz", swaps("gz", 0))
    ffar = lax.ppermute(fsecond, "gz", swaps("gz", 1))
    cfirst, csecond = call(
        functools.partial(pack_corners, dims),
        shapes(corner, corner),
        (left, right, fleft, fright, fnear, ffar),
        0,
        10,
        1,
    )
    cfar = lax.ppermute(csecond, "gz", swaps("gz", 1))
    cnear = lax.ppermute(cfirst, "gz", swaps("gz", 0))

    (count,) = call(
        functools.partial(multiplicity, dims),
        [(tiles, depth + 2 * RING, width + 2 * RING, LANES)],
        (first, near, far, fleft, fright),
        0,
        12,
        8_000_000,
    )
    ext = (tiles + 2, depth + 2 * HALO, width + 2 * RING + 8, LANES)
    (given,) = call(
        functools.partial(assemble, dims),
        [(3,) + ext],
        (u, left, right, fringe, fleft, fright, near, far, fnear, ffar),
        0,
        16,
        8_000_000,
    )
    (out,) = call(
        functools.partial(step_kernel, dims),
        [u.shape],
        (fringe_start, cfar, cnear, count, given),
        1,
        46,
        8_000_000,
        [pltpu.VMEM((n,) + ext, jnp.float32) for n in (3, 3, 3, 6, 3)],
    )
    return out[None]


def solution(mesh):
    placed = (P("box", None, "gz", "gy", None), P("gz", "gy", None), P("gz", "gy"), P())
    return jax.shard_map(
        per_device,
        mesh=mesh,
        in_specs=placed,
        out_specs=P("box", None, "gz", "gy", None),
        check_vma=False,
    )
```
